256 devices in a mesh: dp: 16 (over x_hi, y, core), blk: 16 (over z, x_lo).
Axes of the slice: x: 4 (x_hi: 2, x_lo: 2; x = x_hi * 2 + x_lo), y: 4, z: 8, core: 2. Of those that a mesh axis runs over, the one named last changes fastest.
Arguments:
- rows_in: bfloat16 [16, 16, 16, 16, 4608], P('dp', 'blk'), may hold values from -8 to 8, as said below
- slot_rows: int32 [16, 16, 16, 16], P('dp', 'blk'), may hold values from 0 to 128, as said below
- clip_ids: int32 [16, 2048], P('dp'), may hold values from 0 to 3, never falling along the last dimension, each value on 1 to 2036 neighbouring positions
- clip_reach: int32 [16, 4], P('dp'), may hold values from 0 to 3
- clip_step: int32 [16, 4], P('dp'), may hold values from 0 to 63
- gate_table: bfloat16 [64, 1536], replicated, may hold values from -4 to 4
- out_grad: bfloat16 [16, 2048, 1536], P('dp', 'blk'), may hold values from -6 to 6
Outputs:
- attended: bfloat16 [16, 2048, 1536], P('dp', 'blk')
- qkv_grad: bfloat16 [16, 2048, 4608], P('dp', 'blk')
- gate_grad: float32 [64, 1536], replicated
The draws below stay inside these ranges and needn't reach their ends.
Inputs may be any that keep to these rules, and one draw needn't show every extreme that they name: `rows_in`: each row holds one token's query, key and value columns, 12 heads of 128 side by side in each. For every q and b, the entries below 128 of slot_rows[:, b, q, :] name each of 0 to 127 exactly once; 128 marks an empty slot.
All inputs are finite; a program needn't handle non-finite values.
Results may differ from the reference program's by a relative error of at most 0.023.
Values may be sent and summed in bfloat16 or wider, within the bound.
A program may use at most 128 MiB of HBM per device.

```python
import math
import jax
import jax.numpy as jnp
import numpy as np
from jax import lax

HEADS = 12
HEAD = 128
TOK = 128
FRAME = 128
CLIPS = 4
STEPS = 64
WIDTH = 1536
SEQ = 2048
CAP = 16
N_DP = 16
N_BLK = 16


def draw_rows_in(key, part):
    key = jax.random.fold_in(key, 7)
    row_width = HEADS * HEAD
    full_shape = (N_DP, N_BLK, N_DP, CAP, 3 * row_width)
    column = jnp.arange(3 * row_width)
    value_scale = jnp.where(column >= 2 * row_width, 2.5, 1.6)
    subkeys = jax.random.split(key, 1)
    drawn = jnp.clip(jax.random.normal(subkeys[0], full_shape, jnp.float32), -3.2, 3.2) * value_scale
    return jnp.clip(drawn, -8.0, 8.0).astype(jnp.bfloat16)


def draw_slot_rows(key, part):
    key = jax.random.fold_in(key, 11)
    slot_total = N_DP * CAP
    subkeys = jax.random.split(key, N_BLK * N_DP)
    orders = jax.vmap(lambda single: jax.random.permutation(single, slot_total))(subkeys)
    orders = orders.reshape(N_BLK, N_DP, N_DP, CAP)
    positions = jnp.where(orders < TOK, orders, TOK)
    return jnp.transpose(positions, (2, 0, 1, 3)).astype(jnp.int32)


def set_ends(entries, key, least, high):
    shape = entries.shape
    spot = [jax.random.randint(jax.random.fold_in(key, axis), (), 0, shape[axis]) for axis in range(len(shape))]
    entries = entries.at[tuple(spot)].set(least)
    longest = shape.index(max(shape))
    spot[longest] = (spot[longest] + 1) % shape[longest]
    return entries.at[tuple(spot)].set(high)


def block_scale(own_key, extent, cuts, least, top_value):
    factor_of = 1.0
    for dim, parts in cuts:
        draws = jax.random.uniform(jax.random.fold_in(jax.random.fold_in(own_key, 6), dim), (parts,), jnp.float32, least / len(cuts), top_value / len(cuts))
        factor_of = factor_of * jnp.repeat(jnp.exp(draws), extent[dim] // parts).reshape((-1,) + (1,) * (len(extent) - 1 - dim))
    return factor_of


def split_up(amount, total, bound, skew):
    loads = [(1 << 20) // math.isqrt(rank ** skew) + 1 for rank in range(2, amount + 1)]
    rest, given = total - bound - (amount - 1), [1] * (amount - 1)
    while rest > 0:
        candidates = [i for i in range(amount - 1) if given[i] < bound]
        whole, left = sum([loads[i] for i in candidates]), rest
        for i in candidates:
            more = min(bound - given[i], max(1, left * loads[i] // whole), rest)
            given[i] = given[i] + more
            rest = rest - more
    return np.array([bound] + given)


def ragged(own_key, number_of, total, most, skew):
    if number_of == 2:
        one = jax.random.randint(own_key, (), max(1, total - most), min(most, total - 1) + 1)
        return jnp.stack([one, total - one])
    sizes = jnp.asarray(split_up(number_of, total, most, skew), jnp.int32)
    pairs = (number_of - 1) // 2
    donor, taker = sizes[1:1 + 2 * pairs:2], sizes[2:2 + 2 * pairs:2]
    margin = jnp.minimum(donor - 1, most - taker)
    shifted = jax.random.randint(jax.random.fold_in(own_key, 1), (pairs,), 0, 1 << 20) % (margin + 1)
    sizes = sizes.at[1:1 + 2 * pairs:2].set(donor - shifted).at[2:2 + 2 * pairs:2].set(taker + shifted)
    return sizes[jax.random.permutation(jax.random.fold_in(own_key, 2), number_of)]


def normal_values(key, extent, deviation, bound, cuts=(), kind=jnp.bfloat16):
    array = jax.random.normal(key, extent, jnp.float32) * deviation
    if len(cuts) > 0:
        array = block_scale(key, extent, cuts, -0.22, 0.18) * array
    return jnp.clip(array, min=-bound, max=bound).astype(kind)


def setup_inputs(seed: int = 0) -> dict:
    streams_of = jax.random.split(jax.random.key(seed), 8)
    return {
        "rows_in": draw_rows_in(jax.random.fold_in(streams_of[7], 71), 0),
        "slot_rows": draw_slot_rows(jax.random.fold_in(streams_of[7], 71), 0),
        "clip_ids": jax.vmap(lambda own: jnp.searchsorted(jnp.cumsum(ragged(own, CLIPS, SEQ, SEQ - 3 * CLIPS, 0)), jnp.arange(SEQ), side="right"))(jax.random.split(streams_of[2], N_DP)).reshape((N_DP, SEQ)).astype(jnp.int32),
        "clip_reach": set_ends(jax.random.randint(streams_of[3], (N_DP, CLIPS), 0, 4), jax.random.fold_in(streams_of[3], 1), 0, 3).astype(jnp.int32),
        "clip_step": set_ends(jax.random.randint(streams_of[4], (N_DP, CLIPS), 0, STEPS), jax.random.fold_in(streams_of[4], 1), 0, STEPS - 1).astype(jnp.int32),
        "gate_table": normal_values(streams_of[5], (STEPS, WIDTH), 1.0, 4.0),
        "out_grad": normal_values(streams_of[6], (N_DP, SEQ, WIDTH), 1.0, 6.0, ((0, 16), (1, 16))),
    }


NEGATIVE = -1e+30

def clip_layout(clip_row, reach_row, step_row, frame):
    clip_count = reach_row.shape[0]
    onehot = clip_row[:, None] == jnp.arange(clip_count, dtype=jnp.int32)[None, :]
    counts = lax.optimization_barrier(jnp.sum(onehot.astype(jnp.int32), axis=0))
    starts = jnp.cumsum(counts) - counts
    clip_first = lax.optimization_barrier(jnp.sum(jnp.where(onehot, starts[None, :], 0), axis=1))
    positions = jnp.arange(clip_row.shape[0], dtype=jnp.int32) - clip_first
    mask_block = positions // frame
    row_reach = lax.optimization_barrier(jnp.sum(jnp.where(onehot, reach_row[None, :], 0), axis=1))
    row_step = lax.optimization_barrier(jnp.sum(jnp.where(onehot, step_row[None, :], 0), axis=1))
    return (mask_block, row_reach, row_step)

def allowed_pairs(row_clip, row_block, row_reach, col_clip, col_block):
    same_clip = row_clip[:, None] == col_clip[None, :]
    return same_clip & (col_block[None, :] <= row_block[:, None] + row_reach[:, None])

def placed_rows(rows_in, slot_rows):
    feature = rows_in.shape[-1]
    dest_index = jnp.arange(N_DP, dtype=jnp.int32)[None, None, :, None]
    blk_index = jnp.arange(N_BLK, dtype=jnp.int32)[None, :, None, None]
    target = jnp.where(slot_rows < TOK, dest_index * SEQ + blk_index * TOK + slot_rows, N_DP * SEQ)
    flat_rows = jnp.zeros((N_DP * SEQ, feature), jnp.bfloat16)
    flat_rows = flat_rows.at[target.reshape(-1)].set(rows_in.reshape(-1, feature), mode='drop')
    return flat_rows.reshape(N_DP, SEQ, feature)

def reference(rows_in, slot_rows, clip_ids, clip_reach, clip_step, gate_table, out_grad):
    packed = placed_rows(rows_in, slot_rows)
    row_width = HEADS * HEAD
    score_scale = 1.0 / math.sqrt(HEAD)
    gate_float = gate_table.astype(jnp.float32)

    def split_heads(block_cols):
        return block_cols.reshape(SEQ, HEADS, HEAD).transpose(1, 0, 2)

    def merge_heads(stacked):
        return stacked.transpose(1, 0, 2).reshape(SEQ, row_width)

    def one_group(group_items):
        group_rows, clip_row, reach_row, step_row, grad_rows = group_items
        mask_block, row_reach, row_step = clip_layout(clip_row, reach_row, step_row, FRAME)
        allowed = allowed_pairs(clip_row, mask_block, row_reach, clip_row, mask_block)
        step_hot = (row_step[:, None] == jnp.arange(STEPS, dtype=jnp.int32)[None, :]).astype(jnp.float32)
        gate_rows = jnp.dot(step_hot, gate_float, precision=lax.Precision.HIGHEST)
        grad_float = grad_rows.astype(jnp.float32)
        grad_out = (gate_rows * grad_float).astype(jnp.bfloat16)

        def per_head(head_items):
            queries, key_part, value_part, grad_part = head_items
            scores = jnp.dot(queries, key_part.T, preferred_element_type=jnp.float32) * score_scale
            scores = jnp.where(allowed, scores, NEGATIVE)
            row_top = lax.optimization_barrier(jnp.max(scores, axis=1, keepdims=True))
            log_total = row_top + jnp.log(lax.optimization_barrier(jnp.sum(jnp.exp(scores - row_top), axis=1, keepdims=True)))
            weights = jnp.where(allowed, jnp.exp(scores - log_total), 0.0)
            rounded = weights.astype(jnp.bfloat16)
            attention = jnp.dot(rounded, value_part, preferred_element_type=jnp.float32)
            row_delta = lax.optimization_barrier(jnp.sum(grad_part.astype(jnp.float32) * attention, axis=1, keepdims=True))
            prob_grad = jnp.dot(grad_part, value_part.T, preferred_element_type=jnp.float32)
            score_grad = (weights * (prob_grad - row_delta)).astype(jnp.bfloat16)
            query_grad = jnp.dot(score_grad, key_part, preferred_element_type=jnp.float32) * score_scale
            key_grad = jnp.dot(score_grad.T, queries, preferred_element_type=jnp.float32) * score_scale
            value_grad = jnp.dot(rounded.T, grad_part, preferred_element_type=jnp.float32)
            return (attention, query_grad, key_grad, value_grad)
        head_items = (split_heads(group_rows[:, :row_width]), split_heads(group_rows[:, row_width:2 * row_width]), split_heads(group_rows[:, 2 * row_width:]), split_heads(grad_out))
        attention, query_grad, key_grad, value_grad = lax.map(per_head, head_items)
        attention = merge_heads(attention)
        attended = (gate_rows * attention).astype(jnp.bfloat16)
        qkv_grad = jnp.concatenate([merge_heads(query_grad), merge_heads(key_grad), merge_heads(value_grad)], axis=1).astype(jnp.bfloat16)
        gate_term = jnp.dot(step_hot.T, grad_float * attention, precision=lax.Precision.HIGHEST)
        return (attended, qkv_grad, gate_term)
    attended, qkv_grad, gate_terms = lax.map(one_group, (packed, clip_ids, clip_reach, clip_step, out_grad))
    return (attended, qkv_grad, lax.optimization_barrier(jnp.sum(gate_terms, axis=0)))
```

```python
import math

import jax
import jax.numpy as jnp
from jax import lax
from jax.experimental import pallas as pl
from jax.experimental.pallas import tpu as pltpu
from jax.sharding import PartitionSpec as P

MESH = pl.DeviceIdType.MESH
HEAD = 128
HEADS = 12
WIDTH = HEADS * HEAD
TOK = 128
SEQ = 2048
FRAME = 128
CLIPS = 4
STEPS = 64
CAP = 16
N_DP = 16
N_BLK = 16
N_Z = 8
CHUNKS = 6
SPAN = 3 * HEAD
ROWS = 256
SLOTS = N_DP * CAP
SCALE = 1.0 / math.sqrt(HEAD)
SCALE2 = SCALE * math.log2(math.e)
NEGATIVE = -1e30
ORDER = ((3, 5, 2, 6, 1, 7), (4, 3, 2, 6, 7, 0), (4, 3, 5, 1, 7, 0), (4, 5, 2, 6, 1, 0))


def skip_of(core, x_lo):
    return 3 - 2 * core - x_lo


def order_at(z, skip, k):
    u = lax.rem(skip - z + 8, 4)
    last = jnp.where(u == 2, ORDER[2][k], ORDER[3][k])
    return jnp.where(u == 0, ORDER[0][k], jnp.where(u == 1, ORDER[1][k], last))


def rank_of(z, skip):
    part = lax.rem(z, 4)
    return (z // 4) * 3 + part - jnp.where(part > skip, 1, 0)


def z_of_rank(rank, skip):
    part = lax.rem(rank, 3)
    return (rank // 3) * 4 + part + jnp.where(part >= skip, 1, 0)


def dot(a, b, dims):
    return lax.dot_general(a, b, (dims, ((), ())), preferred_element_type=jnp.float32)


def wait_for(ref, sem):
    pltpu.make_async_copy(ref, ref, sem).wait()


def kernel(
    rows_ref, slot_ref, clip_ref, reach_ref, step_ref, gate_ref, grad_ref,
    att_ref, qkvg_ref, gg_ref,
    stage, recv, slot_src, slot_dst, bsend, qkv, og, weights, dscore, q_t, do_t, cbuf,
    gacc, gpart, g1, g2,
    a_send, a_recv, sl_send, sl_recv, do_send, do_recv, b_send, b_recv, c_send, ca_recv, cq_recv,
    g1s, g1r, g2s, g2r, g3s, g3r,
):
    dp = lax.axis_index("dp")
    blk = lax.axis_index("blk")
    far_x = dp // 8
    y = lax.rem(dp // 2, 4)
    core = lax.rem(dp, 2)
    z = blk // 2
    x_lo = lax.rem(blk, 2)
    skip = skip_of(core, x_lo)
    is_host = lax.rem(z, 4) != skip
    rank = rank_of(z, skip)
    head = x_lo * CHUNKS + rank
    other_core = 1 - core
    other_z = z_of_rank(rank, skip_of(other_core, x_lo))
    other_blk = other_z * 2 + x_lo

    def remote(src, dst, send, arrive, dp_to, blk_to):
        return pltpu.make_async_remote_copy(
            src_ref=src, dst_ref=dst, send_sem=send, recv_sem=arrive,
            device_id=(dp_to, blk_to), device_id_type=MESH,
        )

    barrier = pltpu.get_barrier_semaphore()

    def greet(dp_to, blk_to):
        pl.semaphore_signal(barrier, inc=1, device_id=(dp_to, blk_to), device_id_type=MESH)

    def greet_plane(n, carry):
        greet(lax.rem(dp + n // 2, N_DP), z * 2 + lax.rem(x_lo + n, 2))
        return carry

    def greet_column(n, carry):
        greet(dp, lax.rem(blk + n, N_BLK))
        return carry

    lax.fori_loop(1, 2 * N_DP, greet_plane, 0)
    lax.fori_loop(1, N_BLK, greet_column, 0)

    @pl.when(is_host)
    def _():
        def greet_other(n, carry):
            greet(2 * n + other_core, other_blk)
            return carry

        lax.fori_loop(0, N_DP // 2, greet_other, 0)

    own = core * 8 + dp // 2

    def stage_base(k, x_to, core_to):
        return ((k * 2 + x_to) * 2 + core_to) * 128

    for core_to in (0, 1):
        for k in range(CHUNKS):
            for x_to in (0, 1):
                far = skip_of(core_to, x_to)
                z_to = lax.rem(z + order_at(z, far, k), N_Z)
                column = pl.multiple_of((x_to * CHUNKS + rank_of(z_to, far)) * HEAD, HEAD)
                base = stage_base(k, x_to, core_to)
                for part in range(3):
                    stage[base : base + 128, part * HEAD : (part + 1) * HEAD] = rows_ref[
                        :, core_to, :, pl.ds(part * WIDTH + column, HEAD)
                    ].reshape(128, HEAD)

    lane = lax.broadcasted_iota(jnp.int32, (CAP, SLOTS), 1)
    spread = (lane == lax.broadcasted_iota(jnp.int32, (CAP, SLOTS), 0) + dp * CAP).astype(jnp.bfloat16)
    slots = dot(slot_ref[...].astype(jnp.bfloat16), spread, ((1,), (0,)))
    for q in range(N_DP):
        slot_src[q] = slots[q : q + 1, :]
    source = x_lo * N_DP + dp
    slot_dst[pl.ds(source, 1)] = slot_src[pl.ds(dp, 1)]
    for k in range(CHUNKS):
        recv[pl.ds(pl.multiple_of(k * 512 + source * CAP, CAP), CAP), :] = stage[
            pl.ds(pl.multiple_of(((k * 2 + x_lo) * 16 + own) * CAP, CAP), CAP), :
        ]

    @pl.when(is_host)
    def _():
        og[pl.ds(pl.multiple_of(blk * TOK, TOK), TOK), :] = grad_ref[
            :, pl.ds(pl.multiple_of(head * HEAD, HEAD), HEAD)
        ]
        pl.semaphore_wait(barrier, 2 * N_DP - 1 + N_BLK - 1 + N_DP // 2)

    @pl.when(jnp.logical_not(is_host))
    def _():
        pl.semaphore_wait(barrier, 2 * N_DP - 1 + N_BLK - 1)

    def send_slots(n, carry):
        dp_to = lax.rem(dp + n // 2, N_DP)
        remote(
            slot_src.at[dp_to], slot_dst.at[source], sl_send, sl_recv, dp_to, z * 2 + lax.rem(x_lo + n, 2)
        ).start()
        return carry

    lax.fori_loop(1, 2 * N_DP, send_slots, 0)

    for core_to in (0, 1):
        for k in range(CHUNKS):
            def send_rows(n, carry, core_to=core_to, k=k):
                half = lax.rem(far_x + n // 8, 2) * 4 + lax.rem(y + lax.rem(n // 2, 4), 4)
                x_to = lax.rem(x_lo + n, 2)
                src = ((k * 2 + x_to) * 16 + core_to * 8 + half) * CAP
                remote(
                    stage.at[pl.ds(pl.multiple_of(src, CAP), CAP), :],
                    recv.at[pl.ds(pl.multiple_of(k * 512 + source * CAP, CAP), CAP), :],
                    a_send, a_recv.at[k], half * 2 + core_to, z * 2 + x_to,
                ).start()
                return carry

            lax.fori_loop(1, 16, send_rows, 0)

            @pl.when(core != core_to)
            def _():
                send_rows(0, 0)

            if core_to == 0:
                for x_to in (0, 1):
                    far = skip_of(core, x_to)
                    z_to = lax.rem(z + order_at(z, far, k), N_Z)
                    column = (x_to * CHUNKS + rank_of(z_to, far)) * HEAD
                    blk_to = z_to * 2 + x_to

                    @pl.when(blk_to != blk)
                    def _():
                        remote(
                            grad_ref.at[:, pl.ds(pl.multiple_of(column, HEAD), HEAD)],
                            og.at[pl.ds(pl.multiple_of(blk * TOK, TOK), TOK), :],
                            do_send, do_recv, dp, blk_to,
                        ).start()

    ids = clip_ref[...]
    ends = []
    for c in range(CLIPS):
        ends.append(
            jnp.sum(jnp.where(ids <= c, 1.0, 0.0), axis=1, keepdims=True).astype(jnp.int32)
        )
    starts = [jnp.zeros((1, 1), jnp.int32)] + ends[:-1]

    wait_for(slot_dst.at[pl.ds(0, 31)], sl_recv)
    row_of = lax.broadcasted_iota(jnp.int32, (TOK, SLOTS), 0).astype(jnp.float32)
    placing = []
    for half in range(2):
        slot_row = jnp.sum(slot_dst[half * N_DP : (half + 1) * N_DP], axis=0)
        placing.append(jnp.where(row_of == slot_row, 1.0, 0.0).astype(jnp.bfloat16))
    here = pl.ds(pl.multiple_of(z * ROWS, ROWS), ROWS)
    for k in range(CHUNKS):
        wait_for(recv.at[pl.ds(k * 512, 31 * CAP), :], a_recv.at[k])
        z_to = lax.rem(z + order_at(z, skip, k), N_Z)
        for half in range(2):
            low = k * 512 + half * SLOTS
            bsend[k * ROWS + half * TOK : k * ROWS + (half + 1) * TOK, :] = dot(
                placing[half], recv[low : low + SLOTS, :], ((1,), (0,))
            ).astype(jnp.bfloat16)
        piece = pl.ds(k * ROWS, ROWS)

        @pl.when(z_to != z)
        def _():
            remote(bsend.at[piece, :], qkv.at[here, :], b_send, b_recv, dp, z_to * 2 + x_lo).start()

        @pl.when(z_to == z)
        def _():
            qkv[here, :] = bsend[piece, :]

    @pl.when(is_host)
    def _():
        wait_for(og.at[pl.ds(0, 15 * TOK), :], do_recv)
        wait_for(qkv.at[pl.ds(0, 7 * ROWS), :], b_recv)
        gacc[...] = jnp.zeros((8, HEAD), jnp.float32)
        head_gate = gate_ref[:, pl.ds(pl.multiple_of(head * HEAD, HEAD), HEAD)]

        def send_back(which, z_to, target, column):
            for half in range(2):
                blk_to = z_to * 2 + half
                block = cbuf.at[
                    pl.ds(pl.multiple_of(which * SEQ + z_to * ROWS + half * TOK, TOK), TOK), :
                ]
                place = target.at[:, pl.ds(pl.multiple_of(column * WIDTH + head * HEAD, HEAD), HEAD)]

                @pl.when(blk_to != blk)
                def _():
                    arrive = ca_recv if which == 0 else cq_recv
                    remote(block, place, c_send, arrive, dp, blk_to).start()

                @pl.when(blk_to == blk)
                def _():
                    place[...] = block[...]

        def row_block(n, carry):
            z_to = lax.rem(z + 4 + n, N_Z)
            base = pl.multiple_of(z_to * ROWS, ROWS)
            rows = pl.ds(base, ROWS)
            index = lax.broadcasted_iota(jnp.int32, (ROWS, 1), 0) + base
            low = jnp.zeros((ROWS, 1), jnp.int32)
            high = jnp.zeros((ROWS, 1), jnp.int32)
            step = jnp.zeros((ROWS, 1), jnp.int32)
            inside = []
            for c in range(CLIPS):
                member = (index >= starts[c]) & (index < ends[c])
                inside.append(member)
                stop = starts[c] + ((index - starts[c]) // FRAME + 1 + reach_ref[0, c]) * FRAME
                low = jnp.where(member, starts[c], low)
                high = jnp.where(member, jnp.minimum(stop, ends[c]), high)
                step = jnp.where(member, step_ref[0, c], step)
            queries = qkv[rows, 0:HEAD]
            scores = dot(queries, qkv[:, HEAD : 2 * HEAD], ((1,), (1,)))
            column = lax.broadcasted_iota(jnp.int32, (ROWS, SEQ), 1)
            scores = jnp.where((column >= low) & (column < high), scores, NEGATIVE)
            top = jnp.max(scores, axis=1, keepdims=True)
            parts = jnp.exp2((scores - top) * SCALE2)
            inverse = 1.0 / jnp.sum(parts, axis=1, keepdims=True)
            parts = parts.astype(jnp.bfloat16)
            weights[rows, :] = parts
            attention = dot(parts, qkv[:, 2 * HEAD : 3 * HEAD], ((1,), (0,))) * inverse
            hot = (step == lax.broadcasted_iota(jnp.int32, (ROWS, STEPS), 1)).astype(jnp.bfloat16)
            gate_rows = dot(hot, head_gate, ((1,), (0,)))
            grad = og[rows, :].astype(jnp.float32)
            grad_out = (gate_rows * grad).astype(jnp.bfloat16).astype(jnp.float32)
            cbuf[rows, :] = (gate_rows * attention).astype(jnp.bfloat16)
            send_back(0, z_to, att_ref, 0)
            delta = jnp.sum(grad_out * attention, axis=1, keepdims=True) * inverse
            grad_out = grad_out * inverse
            do_t[:, rows] = grad_out.T.astype(jnp.bfloat16)
            q_t[:, rows] = queries.astype(jnp.float32).T.astype(jnp.bfloat16)
            prob_grad = dot(grad_out.astype(jnp.bfloat16), qkv[:, 2 * HEAD : 3 * HEAD], ((1,), (1,)))
            score_grad = (weights[rows, :].astype(jnp.float32) * (prob_grad - delta)).astype(jnp.bfloat16)
            dscore[rows, :] = score_grad
            query_grad = dot(score_grad, qkv[:, HEAD : 2 * HEAD], ((1,), (0,))) * SCALE
            cbuf[pl.ds(pl.multiple_of(SEQ + base, ROWS), ROWS), :] = query_grad.astype(jnp.bfloat16)
            send_back(1, z_to, qkvg_ref, 0)
            product = grad * attention
            for c in range(CLIPS):
                gacc[c : c + 1, :] += jnp.sum(jnp.where(inside[c], product, 0.0), axis=0, keepdims=True)
            return carry

        lax.fori_loop(0, N_Z, row_block, 0)

        step_row = lax.broadcasted_iota(jnp.int32, (STEPS, HEAD), 0)
        total = jnp.zeros((STEPS, HEAD), jnp.float32)
        for c in range(CLIPS):
            total = total + jnp.where(step_row == step_ref[0, c], gacc[c : c + 1, :], 0.0)
        for p in range(N_DP):
            gpart[p] = total[4 * p : 4 * p + 4, :]
        g1[pl.ds(dp, 1)] = gpart[pl.ds(dp, 1)]

        def send_gate(n, carry):
            dp_to = lax.rem(dp + n, N_DP)
            blk_to = jnp.where(lax.rem(dp_to, 2) == core, blk, other_blk)
            remote(gpart.at[dp_to], g1.at[dp], g1s, g1r, dp_to, blk_to).start()
            return carry

        lax.fori_loop(1, N_DP, send_gate, 0)

        def column_block(n, carry):
            z_to = lax.rem(z + 4 + n, N_Z)
            base = pl.multiple_of(z_to * ROWS, ROWS)
            columns = pl.ds(base, ROWS)
            key_grad = dot(q_t[...], dscore[:, columns], ((1,), (0,))) * SCALE
            cbuf[pl.ds(pl.multiple_of(2 * SEQ + base, ROWS), ROWS), :] = key_grad.T.astype(jnp.bfloat16)
            send_back(2, z_to, qkvg_ref, 1)
            value_grad = dot(do_t[...], weights[:, columns], ((1,), (0,)))
            cbuf[pl.ds(pl.multiple_of(3 * SEQ + base, ROWS), ROWS), :] = value_grad.T.astype(jnp.bfloat16)
            send_back(3, z_to, qkvg_ref, 2)
            return carry

        lax.fori_loop(0, N_Z, column_block, 0)

        wait_for(g1.at[pl.ds(0, 15)], g1r)
        g2[dp, head] = jnp.sum(g1[...], axis=0)

        def send_sum(n, carry):
            mine = g2.at[dp, head]
            remote(mine, mine, g2s, g2r, dp, lax.rem(blk + n, N_BLK)).start()
            return carry

        lax.fori_loop(1, N_BLK, send_sum, 0)
        wait_for(g2.at[dp, pl.ds(0, 11)], g2r)

    @pl.when(jnp.logical_not(is_host))
    def _():
        wait_for(g2.at[dp], g2r)

    def send_steps(n, carry):
        mine = g2.at[dp]
        remote(mine, mine, g3s, g3r, lax.rem(dp + n, N_DP), blk).start()
        return carry

    lax.fori_loop(1, N_DP, send_steps, 0)

    wait_for(slot_dst.at[pl.ds(0, 31)], sl_send)
    wait_for(stage.at[pl.ds(0, 186 * CAP), :], a_send)
    wait_for(g2.at[pl.ds(0, 15)], g3r)
    for p in range(N_DP):
        for h in range(HEADS):
            gg_ref[4 * p : 4 * p + 4, h * HEAD : (h + 1) * HEAD] = g2[p, h]

    @pl.when(is_host)
    def _():
        wait_for(grad_ref.at[:, pl.ds(0, 11 * HEAD)], do_send)
        wait_for(bsend.at[pl.ds(0, 5 * ROWS), :], b_send)
        wait_for(gpart.at[pl.ds(0, 15)], g1s)
        wait_for(gpart.at[pl.ds(0, 15)], g2s)
        wait_for(att_ref.at[:, pl.ds(0, 11 * HEAD)], ca_recv)
        wait_for(qkvg_ref.at[:, pl.ds(0, 33 * HEAD)], cq_recv)
        wait_for(cbuf.at[pl.ds(0, 60 * TOK), :], c_send)

    @pl.when(jnp.logical_not(is_host))
    def _():
        wait_for(grad_ref, do_send)
        wait_for(bsend, b_send)
        wait_for(att_ref, ca_recv)
        wait_for(qkvg_ref, cq_recv)

    wait_for(g2.at[pl.ds(0, 15)], g3s)


def local(rows_in, slot_rows, clip_ids, clip_reach, clip_step, gate_table, out_grad):
    vmem = pl.BlockSpec(memory_space=pltpu.VMEM)
    smem = pl.BlockSpec(memory_space=pltpu.SMEM)
    bf16, f32 = jnp.bfloat16, jnp.float32
    sem = pltpu.SemaphoreType.DMA
    attended, qkv_grad, gate_grad = pl.pallas_call(
        kernel,
        out_shape=(
            jax.ShapeDtypeStruct((TOK, WIDTH), bf16),
            jax.ShapeDtypeStruct((TOK, 3 * WIDTH), bf16),
            jax.ShapeDtypeStruct((STEPS, WIDTH), f32),
        ),
        in_specs=[vmem, vmem, vmem, smem, smem, vmem, vmem],
        out_specs=(vmem, vmem, vmem),
        scratch_shapes=[
            pltpu.VMEM((CHUNKS * 2 * N_DP * CAP, SPAN), bf16),
            pltpu.VMEM((CHUNKS * 2 * SLOTS, SPAN), bf16),
            pltpu.VMEM((N_DP, 1, SLOTS), f32),
            pltpu.VMEM((2 * N_DP, 1, SLOTS), f32),
            pltpu.VMEM((CHUNKS * ROWS, SPAN), bf16),
            pltpu.VMEM((SEQ, SPAN), bf16),
            pltpu.VMEM((SEQ, HEAD), bf16),
            pltpu.VMEM((SEQ, SEQ), bf16),
            pltpu.VMEM((SEQ, SEQ), bf16),
            pltpu.VMEM((HEAD, SEQ), bf16),
            pltpu.VMEM((HEAD, SEQ), bf16),
            pltpu.VMEM((4 * SEQ, HEAD), bf16),
            pltpu.VMEM((8, HEAD), f32),
            pltpu.VMEM((N_DP, 4, HEAD), f32),
            pltpu.VMEM((N_DP, 4, HEAD), f32),
            pltpu.VMEM((N_DP, HEADS, 4, HEAD), f32),
            sem, sem((CHUNKS,)), sem, sem, sem, sem, sem, sem, sem, sem, sem,
            sem, sem, sem, sem, sem, sem,
        ],
        compiler_params=pltpu.CompilerParams(
            collective_id=0, has_side_effects=True, vmem_limit_bytes=56 * 2**20
        ),
        name="attention",
    )(
        rows_in.reshape(8, 2, CAP, 3 * WIDTH),
        slot_rows.reshape(N_DP, CAP),
        clip_ids,
        clip_reach,
        clip_step,
        gate_table,
        out_grad[0],
    )
    return attended[None], qkv_grad[None], gate_grad


def solution(mesh):
    return jax.shard_map(
        local,
        mesh=mesh,
        in_specs=(
            P("dp", "blk", None, None, None),
            P("dp", "blk", None, None),
            P("dp", None),
            P("dp", None),
            P("dp", None),
            P(),
            P("dp", "blk", None),
        ),
        out_specs=(P("dp", "blk", None), P("dp", "blk", None), P()),
        check_vma=False,
    )
```

```python
import math

import jax
import jax.numpy as jnp
from jax import lax
from jax.experimental import pallas as pl
from jax.experimental.pallas import tpu as pltpu
from jax.sharding import PartitionSpec as P

MESH = pl.DeviceIdType.MESH
HEAD = 128
HEADS = 12
WIDTH = HEADS * HEAD
TOK = 128
SEQ = 2048
FRAME = 128
CLIPS = 4
STEPS = 64
CAP = 16
N_DP = 16
N_BLK = 16
N_Z = 8
CHUNKS = 6
SPAN = 3 * HEAD
ROWS = 256
TILE = 512
SLOTS = N_DP * CAP
SCALE = 1.0 / math.sqrt(HEAD)
SCALE2 = SCALE * math.log2(math.e)
NEGATIVE = -1e30
Q0, K0, U0, V0, ONE0 = 0, 128, 256, 384, 512
RETURNS = (4, 3, 5, 2, 6, 1, 7, 0)
ORDER = ((3, 5, 2, 6, 1, 7), (4, 3, 2, 6, 7, 0), (4, 3, 5, 1, 7, 0), (4, 5, 2, 6, 1, 0))


def skip_of(core, x_lo):
    return 3 - 2 * core - x_lo


def order_at(z, skip, k):
    u = lax.rem(skip - z + 8, 4)
    last = jnp.where(u == 2, ORDER[2][k], ORDER[3][k])
    return jnp.where(u == 0, ORDER[0][k], jnp.where(u == 1, ORDER[1][k], last))


def rank_of(z, skip):
    part = lax.rem(z, 4)
    return (z // 4) * 3 + part - jnp.where(part > skip, 1, 0)


def z_of_rank(rank, skip):
    part = lax.rem(rank, 3)
    return (rank // 3) * 4 + part + jnp.where(part >= skip, 1, 0)


def dot(a, b, dims):
    return lax.dot_general(a, b, (dims, ((), ())), preferred_element_type=jnp.float32)


def wait_for(ref, sem):
    pltpu.make_async_copy(ref, ref, sem).wait()


def kernel(
    rows_ref, slot_ref, clip_ref, reach_ref, step_ref, gate_ref, grad_ref,
    att_ref, qkvg_ref, gg_ref,
    stage, recv, slot_src, slot_dst, bsend, wide, og, units, gates, grads, grads_up, step_hot,
    weights, dscore, scores_a, scores_b, q_t, do_t, cbuf, gpart, g1, g2,
    a_send, a_recv, sl_send, sl_recv, do_send, do_recv, b_send, b_recv, c_send, ca_recv, cq_recv,
    g1s, g1r, g2s, g2r, g3s, g3r, go,
):
    dp = lax.axis_index("dp")
    blk = lax.axis_index("blk")
    far_x = dp // 8
    y = lax.rem(dp // 2, 4)
    core = lax.rem(dp, 2)
    z = blk // 2
    x_lo = lax.rem(blk, 2)
    skip = skip_of(core, x_lo)
    is_host = lax.rem(z, 4) != skip
    rank = rank_of(z, skip)
    head = x_lo * CHUNKS + rank
    other_core = 1 - core
    other_z = z_of_rank(rank, skip_of(other_core, x_lo))
    other_blk = other_z * 2 + x_lo

    def remote(src, dst, send, arrive, dp_to, blk_to):
        return pltpu.make_async_remote_copy(
            src_ref=src, dst_ref=dst, send_sem=send, recv_sem=arrive,
            device_id=(dp_to, blk_to), device_id_type=MESH,
        )

    barrier = pltpu.get_barrier_semaphore()

    def greet(dp_to, blk_to):
        pl.semaphore_signal(barrier, inc=1, device_id=(dp_to, blk_to), device_id_type=MESH)

    halves = []
    for n in range(8):
        halves.append(lax.rem(far_x + n // 4, 2) * 4 + lax.rem(y + n % 4, 4))
    x_tos = (x_lo, 1 - x_lo)
    blk_tos = (z * 2 + x_lo, z * 2 + 1 - x_lo)
    plane = [(n, 0) for n in range(1, 16)] + [(n, 1) for n in range(16)]
    cores = (core, 1 - core)
    for n, other in plane:
        greet(halves[n // 2] * 2 + cores[other], blk_tos[n % 2])
    for n in range(1, N_BLK):
        greet(dp, lax.rem(blk + n, N_BLK))

    @pl.when(is_host)
    def _():
        for n in range(8):
            greet(halves[n] * 2 + other_core, other_blk)

    own = core * 8 + dp // 2

    def stage_base(k, x_to, core_to):
        return ((k * 2 + x_to) * 2 + core_to) * 128

    for core_to in (0, 1):
        for k in range(CHUNKS):
            for x_to in (0, 1):
                far = skip_of(core_to, x_to)
                z_to = lax.rem(z + order_at(z, far, k), N_Z)
                column = pl.multiple_of((x_to * CHUNKS + rank_of(z_to, far)) * HEAD, HEAD)
                base = stage_base(k, x_to, core_to)
                for part in range(3):
                    stage[base : base + 128, part * HEAD : (part + 1) * HEAD] = rows_ref[
                        :, core_to, :, pl.ds(part * WIDTH + column, HEAD)
                    ].reshape(128, HEAD)

    lane = lax.broadcasted_iota(jnp.int32, (CAP, SLOTS), 1)
    spread = (lane == lax.broadcasted_iota(jnp.int32, (CAP, SLOTS), 0) + dp * CAP).astype(jnp.bfloat16)
    slots = dot(slot_ref[...].astype(jnp.bfloat16), spread, ((1,), (0,)))
    for q in range(N_DP):
        slot_src[q] = slots[q : q + 1, :]
    source = x_lo * N_DP + dp
    slot_dst[pl.ds(source, 1)] = slot_src[pl.ds(dp, 1)]
    for k in range(CHUNKS):
        recv[pl.ds(pl.multiple_of(k * 512 + source * CAP, CAP), CAP), :] = stage[
            pl.ds(pl.multiple_of(((k * 2 + x_lo) * 16 + own) * CAP, CAP), CAP), :
        ]

    @pl.when(is_host)
    def _():
        og[pl.ds(pl.multiple_of(blk * TOK, TOK), TOK), :] = grad_ref[
            :, pl.ds(pl.multiple_of(head * HEAD, HEAD), HEAD)
        ]
        pl.semaphore_wait(barrier, 2 * N_DP - 1 + N_BLK - 1 + N_DP // 2)

    @pl.when(jnp.logical_not(is_host))
    def _():
        pl.semaphore_wait(barrier, 2 * N_DP - 1 + N_BLK - 1)

    for n, other in plane:
        dp_to = halves[n // 2] * 2 + cores[other]
        remote(slot_src.at[dp_to], slot_dst.at[source], sl_send, sl_recv, dp_to, blk_tos[n % 2]).start()

    source_row = source * CAP
    targets = [x_tos[n % 2] * 256 + halves[n // 2] * CAP for n in range(16)]

    for core_to in (0, 1):
        for k in range(CHUNKS):
            for n in range(16):
                copy = remote(
                    stage.at[pl.ds(pl.multiple_of(targets[n] + (k * 512 + core_to * 128), CAP), CAP), :],
                    recv.at[pl.ds(pl.multiple_of(source_row + k * 512, CAP), CAP), :],
                    a_send, a_recv.at[k], halves[n // 2] * 2 + core_to, blk_tos[n % 2],
                )
                if n:
                    copy.start()
                else:
                    pl.when(core != core_to)(copy.start)

            if core_to == 0:
                for x_to in (0, 1):
                    far = skip_of(core, x_to)
                    z_to = lax.rem(z + order_at(z, far, k), N_Z)
                    column = (x_to * CHUNKS + rank_of(z_to, far)) * HEAD
                    blk_to = z_to * 2 + x_to

                    @pl.when(blk_to != blk)
                    def _():
                        remote(
                            grad_ref.at[:, pl.ds(pl.multiple_of(column, HEAD), HEAD)],
                            og.at[pl.ds(pl.multiple_of(blk * TOK, TOK), TOK), :],
                            do_send, do_recv, dp, blk_to,
                        ).start()

    ids = clip_ref[...]
    ends = []
    for c in range(CLIPS):
        ends.append(
            jnp.sum(jnp.where(ids <= c, 1.0, 0.0), axis=1, keepdims=True).astype(jnp.int32)
        )
    starts = [jnp.zeros((1, 1), jnp.int32)] + ends[:-1]

    @pl.when(is_host)
    def _():
        head_gate = gate_ref[:, pl.ds(pl.multiple_of(head * HEAD, HEAD), HEAD)]
        unit = lax.broadcasted_iota(jnp.int32, (1, HEAD), 1)
        key_low = jnp.full((1, HEAD), SEQ, jnp.int32)
        key_high = jnp.full((1, HEAD), SEQ, jnp.int32)
        row_low = jnp.full((1, HEAD), SEQ, jnp.int32)
        row_high = jnp.full((1, HEAD), SEQ, jnp.int32)
        step_lane = jnp.zeros((1, SEQ), jnp.int32)
        step_of = lax.broadcasted_iota(jnp.int32, (STEPS, HEAD), 0)
        clip_gates = []
        first = jnp.zeros((1, 1), jnp.int32)
        for c in range(CLIPS):
            last = first + (ends[c] - starts[c] + FRAME - 1) // FRAME
            member = (unit >= first) & (unit < last)
            block = unit - first
            key_low = jnp.where(member, starts[c] + block * FRAME, key_low)
            key_high = jnp.where(member, jnp.minimum(starts[c] + block * FRAME + FRAME, ends[c]), key_high)
            row_low = jnp.where(member, starts[c] + jnp.maximum(block - reach_ref[0, c], 0) * FRAME, row_low)
            row_high = jnp.where(member, ends[c], row_high)
            first = last
            step_lane = jnp.where(ids == c, step_ref[0, c], step_lane)
            clip_gates.append(
                jnp.sum(
                    jnp.where(step_of == step_ref[0, c], head_gate.astype(jnp.float32), 0.0),
                    axis=0, keepdims=True,
                )
            )
        step_hot[...] = (
            lax.broadcasted_iota(jnp.int32, (STEPS, SEQ), 0) == step_lane
        ).astype(jnp.bfloat16)
        number = lax.broadcasted_iota(jnp.int32, (ROWS, HEAD), 0)

        def layout(n, carry):
            base = pl.multiple_of(n * ROWS, ROWS)
            rows = pl.ds(base, ROWS)
            index = number + base
            wide[rows, U0 : U0 + HEAD] = jnp.where((index >= key_low) & (index < key_high), 1.0, 0.0).astype(jnp.bfloat16)
            wide[rows, ONE0 : ONE0 + HEAD] = jnp.ones((ROWS, HEAD), jnp.bfloat16)
            units[rows, :] = jnp.where((index >= row_low) & (index < row_high), 0.0, NEGATIVE).astype(jnp.bfloat16)
            gate = clip_gates[CLIPS - 1]
            for c in reversed(range(CLIPS - 1)):
                gate = jnp.where(index < ends[c], clip_gates[c], gate)
            gates[rows, :] = gate.astype(jnp.bfloat16)
            return carry

        lax.fori_loop(0, N_Z, layout, 0)

    wait_for(slot_dst.at[pl.ds(0, 31)], sl_recv)
    row_of = lax.broadcasted_iota(jnp.int32, (TOK, SLOTS), 0).astype(jnp.float32)
    placing = []
    for half in range(2):
        slot_row = jnp.sum(slot_dst[half * N_DP : (half + 1) * N_DP], axis=0)
        placing.append(jnp.where(row_of == slot_row, 1.0, 0.0).astype(jnp.bfloat16))
    here = pl.ds(pl.multiple_of(z * ROWS, ROWS), ROWS)
    for k in range(CHUNKS):
        wait_for(recv.at[pl.ds(k * 512, 31 * CAP), :], a_recv.at[k])
        z_to = lax.rem(z + order_at(z, skip, k), N_Z)
        for half in range(2):
            low = k * 512 + half * SLOTS
            bsend[k * ROWS + half * TOK : k * ROWS + (half + 1) * TOK, :] = dot(
                placing[half], recv[low : low + SLOTS, :], ((1,), (0,))
            ).astype(jnp.bfloat16)
        piece = pl.ds(k * ROWS, ROWS)

        @pl.when(z_to != z)
        def _():
            blk_to = z_to * 2 + x_lo
            remote(
                bsend.at[piece, 0 : 2 * HEAD], wide.at[here, Q0:U0], b_send, b_recv, dp, blk_to
            ).start()
            remote(
                bsend.at[piece, 2 * HEAD : SPAN], wide.at[here, V0:ONE0], b_send, b_recv, dp, blk_to
            ).start()

        @pl.when(z_to == z)
        def _():
            wide[here, Q0:U0] = bsend[piece, 0 : 2 * HEAD]
            wide[here, V0:ONE0] = bsend[piece, 2 * HEAD : SPAN]

    def zs_rows(n, which=0):
        base = lax.rem(z + RETURNS[n], N_Z) * ROWS
        return pl.ds(pl.multiple_of(which * SEQ + base, ROWS), ROWS)

    def send_back(which, n):
        target, column, arrive = (
            (att_ref, 0, ca_recv), (qkvg_ref, 0, cq_recv), (qkvg_ref, 1, cq_recv), (qkvg_ref, 2, cq_recv)
        )[which]
        z_to = lax.rem(z + RETURNS[n], N_Z)
        place = target.at[:, pl.ds(pl.multiple_of(column * WIDTH + head * HEAD, HEAD), HEAD)]
        for half in range(2):
            block = cbuf.at[
                pl.ds(pl.multiple_of(which * SEQ + z_to * ROWS + half * TOK, TOK), TOK), :
            ]
            copy = remote(block, place, c_send, arrive, dp, z_to * 2 + half)
            if RETURNS[n]:
                copy.start()
            else:
                pl.when(half != x_lo)(copy.start)

                @pl.when(half == x_lo)
                def _():
                    place[...] = block[...]

    @pl.when(core == 1)
    def _():
        @pl.when(is_host)
        def _():
            wait_for(bsend.at[pl.ds(0, 5 * ROWS), :], b_send)

        @pl.when(jnp.logical_not(is_host))
        def _():
            wait_for(bsend, b_send)

        pl.semaphore_signal(go, inc=1, device_id=(halves[0] * 2, blk), device_id_type=MESH)

    @pl.when(is_host)
    def _():
        wait_for(og.at[pl.ds(0, 15 * TOK), :], do_recv)
        grads[...] = (gates[...].astype(jnp.float32) * og[...].astype(jnp.float32)).astype(jnp.bfloat16)
        wait_for(recv.at[pl.ds(0, 7 * ROWS), :], b_recv)

        scores = (scores_a, scores_b)

        def score_tile(n, t, queries, top):
            keys = wide[t * TILE : (t + 1) * TILE, K0:V0]
            tile = dot(queries, keys, ((1,), (1,)))
            scores[n % 2][:, t * TILE : (t + 1) * TILE] = tile
            for u in range(TILE // HEAD):
                part = tile[:, u * HEAD : (u + 1) * HEAD]
                top = part if top is None else jnp.maximum(top, part)
            return top

        def query_rows(n):
            return jnp.concatenate([wide[zs_rows(n), Q0:K0], units[zs_rows(n), :]], axis=1)

        lane_of = lax.broadcasted_iota(jnp.int32, (ROWS, HEAD), 1)
        step_total = jnp.zeros((STEPS, HEAD), jnp.float32)
        top = None
        queries = query_rows(0)
        for t in range(SEQ // TILE):
            top = score_tile(0, t, queries, top)
        eye = jnp.where(
            lax.broadcasted_iota(jnp.int32, (HEAD, HEAD), 0) == lax.broadcasted_iota(jnp.int32, (HEAD, HEAD), 1), 1.0, 0.0
        ).astype(jnp.bfloat16)

        def split(rest):
            high = rest.astype(jnp.bfloat16)
            rest = rest - high.astype(jnp.float32)
            middle = rest.astype(jnp.bfloat16)
            return high, middle, (rest - middle.astype(jnp.float32)).astype(jnp.bfloat16)

        def finish_rows(n, summed, step_total):
            rows = zs_rows(n)
            inverse = 1.0 / summed[:, HEAD:]
            attention = summed[:, :HEAD] * inverse
            cbuf[zs_rows(n), :] = (gates[rows, :].astype(jnp.float32) * attention).astype(jnp.bfloat16)
            pl.when(core == 1)(lambda: send_back(0, n))
            grad_out = grads[rows, :].astype(jnp.float32)
            row_delta = jnp.sum(grad_out * attention, axis=1, keepdims=True) * inverse
            grad_out = (grad_out * inverse).astype(jnp.bfloat16)
            high, middle, small = split(-row_delta)
            zero = jnp.zeros((ROWS, HEAD), jnp.bfloat16)
            grads_up[rows, 0:HEAD] = grad_out
            grads_up[rows, HEAD:] = jnp.where(
                lane_of == 0, high, jnp.where(lane_of == 1, middle, jnp.where(lane_of == 2, small, zero))
            )
            do_t[:, rows] = dot(eye, grad_out, ((1,), (1,))).astype(jnp.bfloat16)
            q_t[:, rows] = dot(eye, wide[rows, Q0:K0], ((1,), (1,))).astype(jnp.bfloat16)
            parts = jnp.concatenate(split(og[rows, :].astype(jnp.float32) * attention), axis=1)
            sums = dot(step_hot[:, rows], parts, ((1,), (0,)))
            return step_total + ((sums[:, 2 * HEAD :] + sums[:, HEAD : 2 * HEAD]) + sums[:, :HEAD])

        before = None
        for n in range(N_Z):
            rows = zs_rows(n)
            row_top = jnp.max(top, axis=1, keepdims=True)
            top = None
            if n + 1 < N_Z:
                queries = query_rows(n + 1)
            summed = None
            for t in range(SEQ // TILE):
                columns = slice(t * TILE, (t + 1) * TILE)
                if n + 1 < N_Z:
                    top = score_tile(n + 1, t, queries, top)
                parts = jnp.exp2((scores[n % 2][:, columns] - row_top) * SCALE2).astype(jnp.bfloat16)
                weights[rows, columns] = parts
                term = dot(parts, wide[columns, V0 : V0 + 2 * HEAD], ((1,), (0,)))
                summed = term if summed is None else summed + term
                if t == 0 and before is not None:
                    step_total = finish_rows(n - 1, before, step_total)
            before = summed
        step_total = finish_rows(N_Z - 1, before, step_total)

        for p in range(8):
            gpart[p] = step_total[8 * p : 8 * p + 8, :]
        owner_blk = jnp.where(core == 1, blk, other_blk)
        for n in range(8):
            copy = remote(
                gpart.at[halves[n]], g1.at[dp], g1s, g1r, halves[n] * 2 + 1, owner_blk
            )
            if n:
                copy.start()
            else:
                pl.when(core == 0)(copy.start)

        @pl.when(core == 1)
        def _():
            g1[pl.ds(dp, 1)] = gpart[pl.ds(halves[0], 1)]

        for n in range(N_Z):
            rows = zs_rows(n)
            up = grads_up[rows, :]
            for t in range(SEQ // TILE):
                columns = slice(t * TILE, (t + 1) * TILE)
                prob_grad = dot(up, wide[columns, V0 : V0 + 2 * HEAD], ((1,), (1,)))
                dscore[rows, columns] = (weights[rows, columns].astype(jnp.float32) * prob_grad).astype(jnp.bfloat16)
            query_grad = dot(dscore[rows, :], wide[:, K0:U0], ((1,), (0,))) * SCALE
            cbuf[zs_rows(n, 1), :] = query_grad.astype(jnp.bfloat16)
            pl.when(core == 1)(lambda: send_back(1, n))

        def finish_steps():
            wait_for(g1.at[pl.ds(0, 15)], g1r)
            g2[halves[0], head] = jnp.sum(g1[...], axis=0)
            mine = g2.at[halves[0], head]
            for n in range(1, N_BLK):
                remote(mine, mine, g2s, g2r, dp, lax.rem(blk + n, N_BLK)).start()

        @pl.when(core == 1)
        def _():
            finish_steps()

        for n in range(N_Z):
            columns = zs_rows(n)
            key_grad = dot(q_t[...], dscore[:, columns], ((1,), (0,))) * SCALE
            cbuf[zs_rows(n, 2), :] = key_grad.T.astype(jnp.bfloat16)
            value_grad = dot(do_t[...], weights[:, columns], ((1,), (0,)))
            cbuf[zs_rows(n, 3), :] = value_grad.T.astype(jnp.bfloat16)

            @pl.when(core == 1)
            def _():
                send_back(2, n)
                send_back(3, n)

    @pl.when(core == 0)
    def _():
        pl.semaphore_wait(go, 1)

        @pl.when(is_host)
        def _():
            for n in range(N_Z):
                for which in range(4):
                    send_back(which, n)

    @pl.when(core == 1)
    def _():
        @pl.when(is_host)
        def _():
            wait_for(g2.at[halves[0], pl.ds(0, 11)], g2r)

        @pl.when(jnp.logical_not(is_host))
        def _():
            wait_for(g2.at[halves[0]], g2r)

        mine = g2.at[halves[0]]
        for n in range(16):
            dp_to = halves[n // 2] * 2 + cores[n % 2]
            if n:
                remote(mine, mine, g3s, g3r, dp_to, blk).start()

    wait_for(slot_dst.at[pl.ds(0, 31)], sl_send)
    wait_for(stage.at[pl.ds(0, 186 * CAP), :], a_send)
    @pl.when(core == 0)
    def _():
        wait_for(g2.at[pl.ds(0, 8)], g3r)

    @pl.when(core == 1)
    def _():
        wait_for(g2.at[pl.ds(0, 7)], g3r)

    for p in range(8):
        for h in range(HEADS):
            gg_ref[8 * p : 8 * p + 8, h * HEAD : (h + 1) * HEAD] = g2[p, h]

    @pl.when(is_host)
    def _():
        wait_for(grad_ref.at[:, pl.ds(0, 11 * HEAD)], do_send)

        @pl.when(core == 0)
        def _():
            wait_for(bsend.at[pl.ds(0, 5 * ROWS), :], b_send)


        @pl.when(core == 0)
        def _():
            wait_for(gpart.at[pl.ds(0, 8)], g1s)

        @pl.when(core == 1)
        def _():
            wait_for(gpart.at[pl.ds(0, 7)], g1s)
            wait_for(g1.at[pl.ds(0, 15)], g2s)

        wait_for(att_ref.at[:, pl.ds(0, 11 * HEAD)], ca_recv)
        wait_for(qkvg_ref.at[:, pl.ds(0, 33 * HEAD)], cq_recv)
        wait_for(cbuf.at[pl.ds(0, 60 * TOK), :], c_send)

    @pl.when(jnp.logical_not(is_host))
    def _():
        wait_for(grad_ref, do_send)

        @pl.when(core == 0)
        def _():
            wait_for(bsend, b_send)

        wait_for(att_ref, ca_recv)
        wait_for(qkvg_ref, cq_recv)

    @pl.when(core == 1)
    def _():
        wait_for(stage.at[pl.ds(0, 960), :], g3s)


def local(rows_in, slot_rows, clip_ids, clip_reach, clip_step, gate_table, out_grad):
    vmem = pl.BlockSpec(memory_space=pltpu.VMEM)
    smem = pl.BlockSpec(memory_space=pltpu.SMEM)
    bf16, f32 = jnp.bfloat16, jnp.float32
    sem = pltpu.SemaphoreType.DMA
    attended, qkv_grad, gate_grad = pl.pallas_call(
        kernel,
        out_shape=(
            jax.ShapeDtypeStruct((TOK, WIDTH), bf16),
            jax.ShapeDtypeStruct((TOK, 3 * WIDTH), bf16),
            jax.ShapeDtypeStruct((STEPS, WIDTH), f32),
        ),
        in_specs=[vmem, vmem, vmem, smem, smem, vmem, vmem],
        out_specs=(vmem, vmem, vmem),
        scratch_shapes=[
            pltpu.VMEM((CHUNKS * 2 * N_DP * CAP, SPAN), bf16),
            pltpu.VMEM((CHUNKS * 2 * SLOTS, SPAN), bf16),
            pltpu.VMEM((N_DP, 1, SLOTS), f32),
            pltpu.VMEM((2 * N_DP, 1, SLOTS), f32),
            pltpu.VMEM((CHUNKS * ROWS, SPAN), bf16),
            pltpu.VMEM((SEQ, 5 * HEAD), bf16),
            pltpu.VMEM((SEQ, HEAD), bf16),
            pltpu.VMEM((SEQ, HEAD), bf16),
            pltpu.VMEM((SEQ, HEAD), bf16),
            pltpu.VMEM((SEQ, HEAD), bf16),
            pltpu.VMEM((SEQ, 2 * HEAD), bf16),
            pltpu.VMEM((STEPS, SEQ), bf16),
            pltpu.VMEM((SEQ, SEQ), bf16),
            pltpu.VMEM((SEQ, SEQ), bf16),
            pltpu.VMEM((ROWS, SEQ), f32),
            pltpu.VMEM((ROWS, SEQ), f32),
            pltpu.VMEM((HEAD, SEQ), bf16),
            pltpu.VMEM((HEAD, SEQ), bf16),
            pltpu.VMEM((4 * SEQ, HEAD), bf16),
            pltpu.VMEM((8, 8, HEAD), f32),
            pltpu.VMEM((N_DP, 8, HEAD), f32),
            pltpu.VMEM((8, HEADS, 8, HEAD), f32),
            sem, sem((CHUNKS,)), sem, sem, sem, sem, sem, sem, sem, sem, sem,
            sem, sem, sem, sem, sem, sem, pltpu.SemaphoreType.REGULAR,
        ],
        compiler_params=pltpu.CompilerParams(
            collective_id=0, has_side_effects=True, vmem_limit_bytes=56 * 2**20
        ),
        name="attention",
    )(
        rows_in.reshape(8, 2, CAP, 3 * WIDTH),
        slot_rows.reshape(N_DP, CAP),
        clip_ids,
        clip_reach,
        clip_step,
        gate_table,
        out_grad[0],
    )
    return attended[None], qkv_grad[None], gate_grad


def solution(mesh):
    return jax.shard_map(
        local,
        mesh=mesh,
        in_specs=(
            P("dp", "blk", None, None, None),
            P("dp", "blk", None, None),
            P("dp", None),
            P("dp", None),
            P("dp", None),
            P(),
            P("dp", "blk", None),
        ),
        out_specs=(P("dp", "blk", None), P("dp", "blk", None), P()),
        check_vma=False,
    )
```

```python
import math

import jax
import jax.numpy as jnp
from jax import lax
from jax.experimental import pallas as pl
from jax.experimental.pallas import tpu as pltpu
from jax.sharding import PartitionSpec as P

MESH = pl.DeviceIdType.MESH
HEAD = 128
HEADS = 12
WIDTH = HEADS * HEAD
TOK = 128
SEQ = 2048
FRAME = 128
CLIPS = 4
STEPS = 64
CAP = 16
N_DP = 16
N_BLK = 16
N_Z = 8
CHUNKS = 6
SPAN = 3 * HEAD
ROWS = 256
TILE = 512
SLOTS = N_DP * CAP
SCALE = 1.0 / math.sqrt(HEAD)
SCALE2 = SCALE * math.log2(math.e)
NEGATIVE = -1e30
Q0, K0, U0, V0, ONE0 = 0, 128, 256, 384, 512
RETURNS = (4, 3, 5, 2, 6, 1, 7, 0)
ORDER = ((3, 5, 2, 6, 1, 7), (4, 3, 2, 6, 7, 0), (4, 3, 5, 1, 7, 0), (4, 5, 2, 6, 1, 0))


def skip_of(core, x_lo):
    return 3 - 2 * core - x_lo


def order_at(z, skip, k):
    u = lax.rem(skip - z + 8, 4)
    last = jnp.where(u == 2, ORDER[2][k], ORDER[3][k])
    return jnp.where(u == 0, ORDER[0][k], jnp.where(u == 1, ORDER[1][k], last))


def rank_of(z, skip):
    part = lax.rem(z, 4)
    return (z // 4) * 3 + part - jnp.where(part > skip, 1, 0)


def z_of_rank(rank, skip):
    part = lax.rem(rank, 3)
    return (rank // 3) * 4 + part + jnp.where(part >= skip, 1, 0)


def dot(a, b, dims):
    return lax.dot_general(a, b, (dims, ((), ())), preferred_element_type=jnp.float32)


def wait_for(ref, sem):
    pltpu.make_async_copy(ref, ref, sem).wait()


def kernel(
    rows_ref, slot_ref, clip_ref, reach_ref, step_ref, gate_ref, grad_ref,
    att_ref, qkvg_ref, gg_ref,
    stage, recv, slot_src, slot_dst, bsend, wide, og, units, gates, grads, grads_up, step_hot,
    weights, dscore, scores_a, scores_b, q_t, do_t, cbuf, gpart, g1, g2,
    a_send, a_recv, sl_send, sl_recv, do_send, do_recv, b_send, b_recv, c_send, ca_recv, cq_recv,
    g1s, g1r, g2s, g2r, g3s, g3r,
):
    dp = lax.axis_index("dp")
    blk = lax.axis_index("blk")
    far_x = dp // 8
    y = lax.rem(dp // 2, 4)
    core = lax.rem(dp, 2)
    z = blk // 2
    x_lo = lax.rem(blk, 2)
    skip = skip_of(core, x_lo)
    is_host = lax.rem(z, 4) != skip
    rank = rank_of(z, skip)
    head = x_lo * CHUNKS + rank
    other_core = 1 - core
    other_z = z_of_rank(rank, skip_of(other_core, x_lo))
    other_blk = other_z * 2 + x_lo

    def remote(src, dst, send, arrive, dp_to, blk_to):
        return pltpu.make_async_remote_copy(
            src_ref=src, dst_ref=dst, send_sem=send, recv_sem=arrive,
            device_id=(dp_to, blk_to), device_id_type=MESH,
        )

    barrier = pltpu.get_barrier_semaphore()

    def greet(dp_to, blk_to):
        pl.semaphore_signal(barrier, inc=1, device_id=(dp_to, blk_to), device_id_type=MESH)

    halves = []
    for n in range(8):
        halves.append(lax.rem(far_x + n // 4, 2) * 4 + lax.rem(y + n % 4, 4))
    x_tos = (x_lo, 1 - x_lo)
    blk_tos = (z * 2 + x_lo, z * 2 + 1 - x_lo)
    plane = [(n, 0) for n in range(1, 16)] + [(n, 1) for n in range(16)]
    cores = (core, 1 - core)
    for n, other in plane:
        greet(halves[n // 2] * 2 + cores[other], blk_tos[n % 2])
    for n in range(1, N_BLK):
        greet(dp, lax.rem(blk + n, N_BLK))

    @pl.when(is_host)
    def _():
        for n in range(8):
            greet(halves[n] * 2 + other_core, other_blk)

    own = core * 8 + dp // 2

    def stage_base(k, x_to, core_to):
        return ((k * 2 + x_to) * 2 + core_to) * 128

    for core_to in (0, 1):
        for k in range(CHUNKS):
            for x_to in (0, 1):
                far = skip_of(core_to, x_to)
                z_to = lax.rem(z + order_at(z, far, k), N_Z)
                column = pl.multiple_of((x_to * CHUNKS + rank_of(z_to, far)) * HEAD, HEAD)
                base = stage_base(k, x_to, core_to)
                for part in range(3):
                    stage[base : base + 128, part * HEAD : (part + 1) * HEAD] = rows_ref[
                        :, core_to, :, pl.ds(part * WIDTH + column, HEAD)
                    ].reshape(128, HEAD)

    lane = lax.broadcasted_iota(jnp.int32, (CAP, SLOTS), 1)
    spread = (lane == lax.broadcasted_iota(jnp.int32, (CAP, SLOTS), 0) + dp * CAP).astype(jnp.bfloat16)
    slots = dot(slot_ref[...].astype(jnp.bfloat16), spread, ((1,), (0,)))
    for q in range(N_DP):
        slot_src[q] = slots[q : q + 1, :]
    source = x_lo * N_DP + dp
    slot_dst[pl.ds(source, 1)] = slot_src[pl.ds(dp, 1)]
    for k in range(CHUNKS):
        recv[pl.ds(pl.multiple_of(k * 512 + source * CAP, CAP), CAP), :] = stage[
            pl.ds(pl.multiple_of(((k * 2 + x_lo) * 16 + own) * CAP, CAP), CAP), :
        ]

    @pl.when(is_host)
    def _():
        og[pl.ds(pl.multiple_of(blk * TOK, TOK), TOK), :] = grad_ref[
            :, pl.ds(pl.multiple_of(head * HEAD, HEAD), HEAD)
        ]
        pl.semaphore_wait(barrier, 2 * N_DP - 1 + N_BLK - 1 + N_DP // 2)

    @pl.when(jnp.logical_not(is_host))
    def _():
        pl.semaphore_wait(barrier, 2 * N_DP - 1 + N_BLK - 1)

    for n, other in plane:
        dp_to = halves[n // 2] * 2 + cores[other]
        remote(slot_src.at[dp_to], slot_dst.at[source], sl_send, sl_recv, dp_to, blk_tos[n % 2]).start()

    source_row = source * CAP
    targets = [x_tos[n % 2] * 256 + halves[n // 2] * CAP for n in range(16)]

    for k in range(CHUNKS):
        for core_to in (0, 1):
            for n in range(16):
                copy = remote(
                    stage.at[pl.ds(pl.multiple_of(targets[n] + (k * 512 + core_to * 128), CAP), CAP), :],
                    recv.at[pl.ds(pl.multiple_of(source_row + k * 512, CAP), CAP), :],
                    a_send, a_recv.at[k], halves[n // 2] * 2 + core_to, blk_tos[n % 2],
                )
                if n:
                    copy.start()
                else:
                    pl.when(core != core_to)(copy.start)

            if core_to == 0:
                for x_to in (0, 1):
                    far = skip_of(core, x_to)
                    z_to = lax.rem(z + order_at(z, far, k), N_Z)
                    column = (x_to * CHUNKS + rank_of(z_to, far)) * HEAD
                    blk_to = z_to * 2 + x_to

                    @pl.when(blk_to != blk)
                    def _():
                        remote(
                            grad_ref.at[:, pl.ds(pl.multiple_of(column, HEAD), HEAD)],
                            og.at[pl.ds(pl.multiple_of(blk * TOK, TOK), TOK), :],
                            do_send, do_recv, dp, blk_to,
                        ).start()

    ids = clip_ref[...]
    ends = []
    for c in range(CLIPS):
        ends.append(
            jnp.sum(jnp.where(ids <= c, 1.0, 0.0), axis=1, keepdims=True).astype(jnp.int32)
        )
    starts = [jnp.zeros((1, 1), jnp.int32)] + ends[:-1]

    @pl.when(is_host)
    def _():
        head_gate = gate_ref[:, pl.ds(pl.multiple_of(head * HEAD, HEAD), HEAD)]
        unit = lax.broadcasted_iota(jnp.int32, (1, HEAD), 1)
        key_low = jnp.full((1, HEAD), SEQ, jnp.int32)
        key_high = jnp.full((1, HEAD), SEQ, jnp.int32)
        row_low = jnp.full((1, HEAD), SEQ, jnp.int32)
        row_high = jnp.full((1, HEAD), SEQ, jnp.int32)
        step_lane = jnp.zeros((1, SEQ), jnp.int32)
        step_of = lax.broadcasted_iota(jnp.int32, (STEPS, HEAD), 0)
        clip_gates = []
        first = jnp.zeros((1, 1), jnp.int32)
        for c in range(CLIPS):
            last = first + (ends[c] - starts[c] + FRAME - 1) // FRAME
            member = (unit >= first) & (unit < last)
            block = unit - first
            key_low = jnp.where(member, starts[c] + block * FRAME, key_low)
            key_high = jnp.where(member, jnp.minimum(starts[c] + block * FRAME + FRAME, ends[c]), key_high)
            row_low = jnp.where(member, starts[c] + jnp.maximum(block - reach_ref[0, c], 0) * FRAME, row_low)
            row_high = jnp.where(member, ends[c], row_high)
            first = last
            step_lane = jnp.where(ids == c, step_ref[0, c], step_lane)
            clip_gates.append(
                jnp.sum(
                    jnp.where(step_of == step_ref[0, c], head_gate.astype(jnp.float32), 0.0),
                    axis=0, keepdims=True,
                )
            )
        step_hot[...] = (
            lax.broadcasted_iota(jnp.int32, (STEPS, SEQ), 0) == step_lane
        ).astype(jnp.bfloat16)
        number = lax.broadcasted_iota(jnp.int32, (ROWS, HEAD), 0)

        def layout(n, carry):
            base = pl.multiple_of(n * ROWS, ROWS)
            rows = pl.ds(base, ROWS)
            index = number + base
            wide[rows, U0 : U0 + HEAD] = jnp.where((index >= key_low) & (index < key_high), 1.0, 0.0).astype(jnp.bfloat16)
            wide[rows, ONE0 : ONE0 + HEAD] = jnp.ones((ROWS, HEAD), jnp.bfloat16)
            units[rows, :] = jnp.where((index >= row_low) & (index < row_high), 0.0, NEGATIVE).astype(jnp.bfloat16)
            gate = clip_gates[CLIPS - 1]
            for c in reversed(range(CLIPS - 1)):
                gate = jnp.where(index < ends[c], clip_gates[c], gate)
            gates[rows, :] = gate.astype(jnp.bfloat16)
            return carry

        lax.fori_loop(0, N_Z, layout, 0)

    wait_for(slot_dst.at[pl.ds(0, 31)], sl_recv)
    row_of = lax.broadcasted_iota(jnp.int32, (TOK, SLOTS), 0).astype(jnp.float32)
    placing = []
    for half in range(2):
        slot_row = jnp.sum(slot_dst[half * N_DP : (half + 1) * N_DP], axis=0)
        placing.append(jnp.where(row_of == slot_row, 1.0, 0.0).astype(jnp.bfloat16))
    here = pl.ds(pl.multiple_of(z * ROWS, ROWS), ROWS)
    for k in range(CHUNKS):
        wait_for(recv.at[pl.ds(k * 512, 31 * CAP), :], a_recv.at[k])
        z_to = lax.rem(z + order_at(z, skip, k), N_Z)
        for half in range(2):
            low = k * 512 + half * SLOTS
            bsend[k * ROWS + half * TOK : k * ROWS + (half + 1) * TOK, :] = dot(
                placing[half], recv[low : low + SLOTS, :], ((1,), (0,))
            ).astype(jnp.bfloat16)
        piece = pl.ds(k * ROWS, ROWS)

        @pl.when(z_to != z)
        def _():
            blk_to = z_to * 2 + x_lo
            remote(
                bsend.at[piece, 0 : 2 * HEAD], wide.at[here, Q0:U0], b_send, b_recv, dp, blk_to
            ).start()
            remote(
                bsend.at[piece, 2 * HEAD : SPAN], wide.at[here, V0:ONE0], b_send, b_recv, dp, blk_to
            ).start()

        @pl.when(z_to == z)
        def _():
            wide[here, Q0:U0] = bsend[piece, 0 : 2 * HEAD]
            wide[here, V0:ONE0] = bsend[piece, 2 * HEAD : SPAN]

    def zs_rows(n, which=0):
        base = lax.rem(z + RETURNS[n], N_Z) * ROWS
        return pl.ds(pl.multiple_of(which * SEQ + base, ROWS), ROWS)

    def send_back(which, n):
        target, column, arrive = (
            (att_ref, 0, ca_recv), (qkvg_ref, 0, cq_recv), (qkvg_ref, 1, cq_recv), (qkvg_ref, 2, cq_recv)
        )[which]
        z_to = lax.rem(z + RETURNS[n], N_Z)
        place = target.at[:, pl.ds(pl.multiple_of(column * WIDTH + head * HEAD, HEAD), HEAD)]
        for half in range(2):
            block = cbuf.at[
                pl.ds(pl.multiple_of(which * SEQ + z_to * ROWS + half * TOK, TOK), TOK), :
            ]
            copy = remote(block, place, c_send, arrive, dp, z_to * 2 + half)
            if RETURNS[n]:
                copy.start()
            else:
                pl.when(half != x_lo)(copy.start)

                @pl.when(half == x_lo)
                def _():
                    place[...] = block[...]

    @pl.when(is_host)
    def _():
        wait_for(og.at[pl.ds(0, 15 * TOK), :], do_recv)
        grads[...] = (gates[...].astype(jnp.float32) * og[...].astype(jnp.float32)).astype(jnp.bfloat16)
        wait_for(recv.at[pl.ds(0, 7 * ROWS), :], b_recv)

        scores = (scores_a, scores_b)

        def score_tile(n, t, queries, top):
            keys = wide[t * TILE : (t + 1) * TILE, K0:V0]
            tile = dot(queries, keys, ((1,), (1,)))
            scores[n % 2][:, t * TILE : (t + 1) * TILE] = tile
            for u in range(TILE // HEAD):
                part = tile[:, u * HEAD : (u + 1) * HEAD]
                top = part if top is None else jnp.maximum(top, part)
            return top

        def query_rows(n):
            return jnp.concatenate([wide[zs_rows(n), Q0:K0], units[zs_rows(n), :]], axis=1)

        lane_of = lax.broadcasted_iota(jnp.int32, (ROWS, HEAD), 1)
        step_total = jnp.zeros((STEPS, HEAD), jnp.float32)
        top = None
        queries = query_rows(0)
        for t in range(SEQ // TILE):
            top = score_tile(0, t, queries, top)
        eye = jnp.where(
            lax.broadcasted_iota(jnp.int32, (HEAD, HEAD), 0) == lax.broadcasted_iota(jnp.int32, (HEAD, HEAD), 1), 1.0, 0.0
        ).astype(jnp.bfloat16)

        def split(rest):
            high = rest.astype(jnp.bfloat16)
            rest = rest - high.astype(jnp.float32)
            middle = rest.astype(jnp.bfloat16)
            return high, middle, (rest - middle.astype(jnp.float32)).astype(jnp.bfloat16)

        def finish_rows(n, summed, step_total):
            rows = zs_rows(n)
            inverse = 1.0 / summed[:, HEAD:]
            attention = summed[:, :HEAD] * inverse
            cbuf[zs_rows(n), :] = (gates[rows, :].astype(jnp.float32) * attention).astype(jnp.bfloat16)
            send_back(0, n)
            grad_out = grads[rows, :].astype(jnp.float32)
            row_delta = jnp.sum(grad_out * attention, axis=1, keepdims=True) * inverse
            grad_out = (grad_out * inverse).astype(jnp.bfloat16)
            high, middle, small = split(-row_delta)
            zero = jnp.zeros((ROWS, HEAD), jnp.bfloat16)
            grads_up[rows, 0:HEAD] = grad_out
            grads_up[rows, HEAD:] = jnp.where(
                lane_of == 0, high, jnp.where(lane_of == 1, middle, jnp.where(lane_of == 2, small, zero))
            )
            do_t[:, rows] = dot(eye, grad_out, ((1,), (1,))).astype(jnp.bfloat16)
            q_t[:, rows] = dot(eye, wide[rows, Q0:K0], ((1,), (1,))).astype(jnp.bfloat16)
            parts = jnp.concatenate(split(og[rows, :].astype(jnp.float32) * attention), axis=1)
            sums = dot(step_hot[:, rows], parts, ((1,), (0,)))
            return step_total + ((sums[:, 2 * HEAD :] + sums[:, HEAD : 2 * HEAD]) + sums[:, :HEAD])

        before = None
        for n in range(N_Z):
            rows = zs_rows(n)
            row_top = jnp.max(top, axis=1, keepdims=True)
            top = None
            if n + 1 < N_Z:
                queries = query_rows(n + 1)
            summed = None
            for t in range(SEQ // TILE):
                columns = slice(t * TILE, (t + 1) * TILE)
                if n + 1 < N_Z:
                    top = score_tile(n + 1, t, queries, top)
                parts = jnp.exp2((scores[n % 2][:, columns] - row_top) * SCALE2).astype(jnp.bfloat16)
                weights[rows, columns] = parts
                term = dot(parts, wide[columns, V0 : V0 + 2 * HEAD], ((1,), (0,)))
                summed = term if summed is None else summed + term
                if t == 0 and before is not None:
                    step_total = finish_rows(n - 1, before, step_total)
            before = summed
        step_total = finish_rows(N_Z - 1, before, step_total)

        for p in range(8):
            gpart[p] = step_total[8 * p : 8 * p + 8, :]
        owner_blk = jnp.where(core == 1, blk, other_blk)
        for n in range(8):
            copy = remote(
                gpart.at[halves[n]], g1.at[dp], g1s, g1r, halves[n] * 2 + 1, owner_blk
            )
            if n:
                copy.start()
            else:
                pl.when(core == 0)(copy.start)

        @pl.when(core == 1)
        def _():
            g1[pl.ds(dp, 1)] = gpart[pl.ds(halves[0], 1)]

        for n in range(N_Z):
            rows = zs_rows(n)
            up = grads_up[rows, :]
            for t in range(SEQ // TILE):
                columns = slice(t * TILE, (t + 1) * TILE)
                prob_grad = dot(up, wide[columns, V0 : V0 + 2 * HEAD], ((1,), (1,)))
                dscore[rows, columns] = (weights[rows, columns].astype(jnp.float32) * prob_grad).astype(jnp.bfloat16)
            query_grad = dot(dscore[rows, :], wide[:, K0:U0], ((1,), (0,))) * SCALE
            cbuf[zs_rows(n, 1), :] = query_grad.astype(jnp.bfloat16)
            send_back(1, n)

        def finish_steps():
            wait_for(g1.at[pl.ds(0, 15)], g1r)
            g2[halves[0], head] = jnp.sum(g1[...], axis=0)
            mine = g2.at[halves[0], head]
            for n in range(1, N_BLK):
                remote(mine, mine, g2s, g2r, dp, lax.rem(blk + n, N_BLK)).start()

        @pl.when(core == 1)
        def _():
            finish_steps()

        for n in range(N_Z):
            columns = zs_rows(n)
            key_grad = dot(q_t[...], dscore[:, columns], ((1,), (0,))) * SCALE
            cbuf[zs_rows(n, 2), :] = key_grad.T.astype(jnp.bfloat16)
            value_grad = dot(do_t[...], weights[:, columns], ((1,), (0,)))
            cbuf[zs_rows(n, 3), :] = value_grad.T.astype(jnp.bfloat16)

            send_back(2, n)
            send_back(3, n)

    @pl.when(core == 1)
    def _():
        @pl.when(is_host)
        def _():
            wait_for(g2.at[halves[0], pl.ds(0, 11)], g2r)

        @pl.when(jnp.logical_not(is_host))
        def _():
            wait_for(g2.at[halves[0]], g2r)

        mine = g2.at[halves[0]]
        for n in range(16):
            dp_to = halves[n // 2] * 2 + cores[n % 2]
            if n:
                remote(mine, mine, g3s, g3r, dp_to, blk).start()

    wait_for(slot_dst.at[pl.ds(0, 31)], sl_send)
    wait_for(stage.at[pl.ds(0, 186 * CAP), :], a_send)
    @pl.when(core == 0)
    def _():
        wait_for(g2.at[pl.ds(0, 8)], g3r)

    @pl.when(core == 1)
    def _():
        wait_for(g2.at[pl.ds(0, 7)], g3r)

    for p in range(8):
        for h in range(HEADS):
            gg_ref[8 * p : 8 * p + 8, h * HEAD : (h + 1) * HEAD] = g2[p, h]

    @pl.when(is_host)
    def _():
        wait_for(grad_ref.at[:, pl.ds(0, 11 * HEAD)], do_send)
        wait_for(bsend.at[pl.ds(0, 5 * ROWS), :], b_send)

        @pl.when(core == 0)
        def _():
            wait_for(gpart.at[pl.ds(0, 8)], g1s)

        @pl.when(core == 1)
        def _():
            wait_for(gpart.at[pl.ds(0, 7)], g1s)
            wait_for(g1.at[pl.ds(0, 15)], g2s)

        wait_for(att_ref.at[:, pl.ds(0, 11 * HEAD)], ca_recv)
        wait_for(qkvg_ref.at[:, pl.ds(0, 33 * HEAD)], cq_recv)
        wait_for(cbuf.at[pl.ds(0, 60 * TOK), :], c_send)

    @pl.when(jnp.logical_not(is_host))
    def _():
        wait_for(grad_ref, do_send)
        wait_for(bsend, b_send)
        wait_for(att_ref, ca_recv)
        wait_for(qkvg_ref, cq_recv)

    @pl.when(core == 1)
    def _():
        wait_for(stage.at[pl.ds(0, 960), :], g3s)


def settle(a, b, c, a_out, b_out, c_out):
    a_out[...] = a[...]
    b_out[...] = b[...]
    c_out[...] = c[...]


def local(rows_in, slot_rows, clip_ids, clip_reach, clip_step, gate_table, out_grad):
    vmem = pl.BlockSpec(memory_space=pltpu.VMEM)
    smem = pl.BlockSpec(memory_space=pltpu.SMEM)
    bf16, f32 = jnp.bfloat16, jnp.float32
    sem = pltpu.SemaphoreType.DMA
    attended, qkv_grad, gate_grad = pl.pallas_call(
        kernel,
        out_shape=(
            jax.ShapeDtypeStruct((TOK, WIDTH), bf16),
            jax.ShapeDtypeStruct((TOK, 3 * WIDTH), bf16),
            jax.ShapeDtypeStruct((STEPS, WIDTH), f32),
        ),
        in_specs=[vmem, vmem, vmem, smem, smem, vmem, vmem],
        out_specs=(vmem, vmem, vmem),
        scratch_shapes=[
            pltpu.VMEM((CHUNKS * 2 * N_DP * CAP, SPAN), bf16),
            pltpu.VMEM((CHUNKS * 2 * SLOTS, SPAN), bf16),
            pltpu.VMEM((N_DP, 1, SLOTS), f32),
            pltpu.VMEM((2 * N_DP, 1, SLOTS), f32),
            pltpu.VMEM((CHUNKS * ROWS, SPAN), bf16),
            pltpu.VMEM((SEQ, 5 * HEAD), bf16),
            pltpu.VMEM((SEQ, HEAD), bf16),
            pltpu.VMEM((SEQ, HEAD), bf16),
            pltpu.VMEM((SEQ, HEAD), bf16),
            pltpu.VMEM((SEQ, HEAD), bf16),
            pltpu.VMEM((SEQ, 2 * HEAD), bf16),
            pltpu.VMEM((STEPS, SEQ), bf16),
            pltpu.VMEM((SEQ, SEQ), bf16),
            pltpu.VMEM((SEQ, SEQ), bf16),
            pltpu.VMEM((ROWS, SEQ), f32),
            pltpu.VMEM((ROWS, SEQ), f32),
            pltpu.VMEM((HEAD, SEQ), bf16),
            pltpu.VMEM((HEAD, SEQ), bf16),
            pltpu.VMEM((4 * SEQ, HEAD), bf16),
            pltpu.VMEM((8, 8, HEAD), f32),
            pltpu.VMEM((N_DP, 8, HEAD), f32),
            pltpu.VMEM((8, HEADS, 8, HEAD), f32),
            sem, sem((CHUNKS,)), sem, sem, sem, sem, sem, sem, sem, sem, sem,
            sem, sem, sem, sem, sem, sem,
        ],
        compiler_params=pltpu.CompilerParams(
            collective_id=0, has_side_effects=True, vmem_limit_bytes=56 * 2**20
        ),
        name="attention",
    )(
        rows_in.reshape(8, 2, CAP, 3 * WIDTH),
        slot_rows.reshape(N_DP, CAP),
        clip_ids,
        clip_reach,
        clip_step,
        gate_table,
        out_grad[0],
    )
    shapes = [x.shape for x in (attended, qkv_grad, gate_grad)]
    blocks = [pl.BlockSpec((rows // 4, columns), lambda i: (i, 0)) for rows, columns in shapes]
    attended, qkv_grad, gate_grad = pl.pallas_call(
        settle,
        grid=(4,),
        out_shape=tuple(jax.ShapeDtypeStruct(x.shape, x.dtype) for x in (attended, qkv_grad, gate_grad)),
        in_specs=blocks,
        out_specs=tuple(blocks),
        name="settle",
    )(attended, qkv_grad, gate_grad)
    return attended[None], qkv_grad[None], gate_grad


def solution(mesh):
    return jax.shard_map(
        local,
        mesh=mesh,
        in_specs=(
            P("dp", "blk", None, None, None),
            P("dp", "blk", None, None),
            P("dp", None),
            P("dp", None),
            P("dp", None),
            P(),
            P("dp", "blk", None),
        ),
        out_specs=(P("dp", "blk", None), P("dp", "blk", None), P()),
        check_vma=False,
    )
```

```python
import math

import jax
import jax.numpy as jnp
from jax import lax
from jax.experimental import pallas as pl
from jax.experimental.pallas import tpu as pltpu
from jax.sharding import PartitionSpec as P

MESH = pl.DeviceIdType.MESH
HEAD = 128
HEADS = 12
WIDTH = HEADS * HEAD
TOK = 128
SEQ = 2048
FRAME = 128
CLIPS = 4
STEPS = 64
CAP = 16
N_DP = 16
N_BLK = 16
N_Z = 8
CHUNKS = 6
SPAN = 3 * HEAD
ROWS = 256
TILE = 512
SLOTS = N_DP * CAP
SCALE = 1.0 / math.sqrt(HEAD)
SCALE2 = SCALE * math.log2(math.e)
NEGATIVE = -1e30
Q0, K0, U0, V0, ONE0 = 0, 128, 256, 384, 512
GATE_AT = 4
RETURNS = (4, 3, 5, 2, 6, 1, 7, 0)
ORDER = ((3, 5, 2, 6, 1, 7), (4, 3, 2, 6, 7, 0), (4, 3, 5, 1, 7, 0), (4, 5, 2, 6, 1, 0))


def skip_of(core, x_lo):
    return 3 - 2 * core - x_lo


def order_at(z, skip, k):
    u = lax.rem(skip - z + 8, 4)
    last = jnp.where(u == 2, ORDER[2][k], ORDER[3][k])
    return jnp.where(u == 0, ORDER[0][k], jnp.where(u == 1, ORDER[1][k], last))


def rank_of(z, skip):
    part = lax.rem(z, 4)
    return (z // 4) * 3 + part - jnp.where(part > skip, 1, 0)


def z_of_rank(rank, skip):
    part = lax.rem(rank, 3)
    return (rank // 3) * 4 + part + jnp.where(part >= skip, 1, 0)


def dot(a, b, dims):
    return lax.dot_general(a, b, (dims, ((), ())), preferred_element_type=jnp.float32)


def wait_for(ref, sem):
    pltpu.make_async_copy(ref, ref, sem).wait()


def kernel(
    rows_ref, slot_ref, clip_ref, reach_ref, step_ref, gate_ref, grad_ref,
    att_ref, qkvg_ref, gg_ref,
    rows_here, in_sem, stage, recv, slot_src, slot_dst, bsend, wide, og, units, gates, grads, grads_up, step_hot,
    weights, dscore, scores_a, scores_b, q_t, do_t, cbuf, gpart, g1, g2,
    a_send, a_recv, sl_send, sl_recv, do_send, do_recv, b_send, b_recv, c_send, ca_recv, cq_recv,
    g1s, g1r, g2s, g2r, g3s, g3r, hop,
):
    for n in range(8):
        pltpu.make_async_copy(rows_ref.at[n], rows_here.at[n], in_sem).start()
    dp = lax.axis_index("dp")
    blk = lax.axis_index("blk")
    far_x = dp // 8
    y = lax.rem(dp // 2, 4)
    core = lax.rem(dp, 2)
    z = blk // 2
    x_lo = lax.rem(blk, 2)
    skip = skip_of(core, x_lo)
    is_host = lax.rem(z, 4) != skip
    rank = rank_of(z, skip)
    head = x_lo * CHUNKS + rank
    other_core = 1 - core
    other_z = z_of_rank(rank, skip_of(other_core, x_lo))
    other_blk = other_z * 2 + x_lo

    def remote(src, dst, send, arrive, dp_to, blk_to):
        return pltpu.make_async_remote_copy(
            src_ref=src, dst_ref=dst, send_sem=send, recv_sem=arrive,
            device_id=(dp_to, blk_to), device_id_type=MESH,
        )

    barrier = pltpu.get_barrier_semaphore()

    def greet(dp_to, blk_to):
        pl.semaphore_signal(barrier, inc=1, device_id=(dp_to, blk_to), device_id_type=MESH)

    halves = []
    for n in range(8):
        halves.append(lax.rem(far_x + n // 4, 2) * 4 + lax.rem(y + n % 4, 4))
    x_tos = (x_lo, 1 - x_lo)
    blk_tos = (z * 2 + x_lo, z * 2 + 1 - x_lo)
    plane = [(n, 0) for n in range(1, 16)] + [(n, 1) for n in range(16)]
    cores = (core, 1 - core)
    for n, other in plane:
        greet(halves[n // 2] * 2 + cores[other], blk_tos[n % 2])
    for n in range(1, N_BLK):
        greet(dp, lax.rem(blk + n, N_BLK))

    @pl.when(is_host)
    def _():
        for n in range(8):
            greet(halves[n] * 2 + other_core, other_blk)

    own = core * 8 + dp // 2

    def stage_base(k, x_to, core_to):
        return ((k * 2 + x_to) * 2 + core_to) * 128

    wait_for(rows_here, in_sem)
    for core_to in (0, 1):
        for k in range(CHUNKS):
            for x_to in (0, 1):
                far = skip_of(core_to, x_to)
                z_to = lax.rem(z + order_at(z, far, k), N_Z)
                column = pl.multiple_of((x_to * CHUNKS + rank_of(z_to, far)) * HEAD, HEAD)
                base = stage_base(k, x_to, core_to)
                for part in range(3):
                    stage[base : base + 128, part * HEAD : (part + 1) * HEAD] = rows_here[
                        :, core_to, :, pl.ds(part * WIDTH + column, HEAD)
                    ].reshape(128, HEAD)

    lane = lax.broadcasted_iota(jnp.int32, (CAP, SLOTS), 1)
    spread = (lane == lax.broadcasted_iota(jnp.int32, (CAP, SLOTS), 0) + dp * CAP).astype(jnp.bfloat16)
    slots = dot(slot_ref[...].astype(jnp.bfloat16), spread, ((1,), (0,)))
    for q in range(N_DP):
        slot_src[q] = slots[q : q + 1, :]
    source = x_lo * N_DP + dp
    slot_dst[pl.ds(source, 1)] = slot_src[pl.ds(dp, 1)]
    for k in range(CHUNKS):
        recv[pl.ds(pl.multiple_of(k * 512 + source * CAP, CAP), CAP), :] = stage[
            pl.ds(pl.multiple_of(((k * 2 + x_lo) * 16 + own) * CAP, CAP), CAP), :
        ]

    @pl.when(is_host)
    def _():
        og[pl.ds(pl.multiple_of(blk * TOK, TOK), TOK), :] = grad_ref[
            :, pl.ds(pl.multiple_of(head * HEAD, HEAD), HEAD)
        ]
        pl.semaphore_wait(barrier, 2 * N_DP - 1 + N_BLK - 1 + N_DP // 2)

    @pl.when(jnp.logical_not(is_host))
    def _():
        pl.semaphore_wait(barrier, 2 * N_DP - 1 + N_BLK - 1)

    for n, other in plane:
        dp_to = halves[n // 2] * 2 + cores[other]
        remote(slot_src.at[dp_to], slot_dst.at[source], sl_send, sl_recv, dp_to, blk_tos[n % 2]).start()

    source_row = source * CAP
    targets = [x_tos[n % 2] * 256 + halves[n // 2] * CAP for n in range(16)]

    for k in range(CHUNKS):
        for core_to in (0, 1):
            for n in range(16):
                copy = remote(
                    stage.at[pl.ds(pl.multiple_of(targets[n] + (k * 512 + core_to * 128), CAP), CAP), :],
                    recv.at[pl.ds(pl.multiple_of(source_row + k * 512, CAP), CAP), :],
                    a_send, a_recv.at[k], halves[n // 2] * 2 + core_to, blk_tos[n % 2],
                )
                if n:
                    copy.start()
                else:
                    pl.when(core != core_to)(copy.start)

            if core_to == 0:
                for x_to in (0, 1):
                    far = skip_of(core, x_to)
                    z_to = lax.rem(z + order_at(z, far, k), N_Z)
                    column = (x_to * CHUNKS + rank_of(z_to, far)) * HEAD
                    blk_to = z_to * 2 + x_to

                    @pl.when(blk_to != blk)
                    def _():
                        remote(
                            grad_ref.at[:, pl.ds(pl.multiple_of(column, HEAD), HEAD)],
                            og.at[pl.ds(pl.multiple_of(blk * TOK, TOK), TOK), :],
                            do_send, do_recv, dp, blk_to,
                        ).start()

    ids = clip_ref[...]
    ends = []
    for c in range(CLIPS):
        ends.append(
            jnp.sum(jnp.where(ids <= c, 1.0, 0.0), axis=1, keepdims=True).astype(jnp.int32)
        )
    starts = [jnp.zeros((1, 1), jnp.int32)] + ends[:-1]

    @pl.when(is_host)
    def _():
        head_gate = gate_ref[:, pl.ds(pl.multiple_of(head * HEAD, HEAD), HEAD)]
        unit = lax.broadcasted_iota(jnp.int32, (1, HEAD), 1)
        key_low = jnp.full((1, HEAD), SEQ, jnp.int32)
        key_high = jnp.full((1, HEAD), SEQ, jnp.int32)
        row_low = jnp.full((1, HEAD), SEQ, jnp.int32)
        row_high = jnp.full((1, HEAD), SEQ, jnp.int32)
        step_lane = jnp.zeros((1, SEQ), jnp.int32)
        step_of = lax.broadcasted_iota(jnp.int32, (STEPS, HEAD), 0)
        clip_gates = []
        first = jnp.zeros((1, 1), jnp.int32)
        for c in range(CLIPS):
            last = first + (ends[c] - starts[c] + FRAME - 1) // FRAME
            member = (unit >= first) & (unit < last)
            block = unit - first
            key_low = jnp.where(member, starts[c] + block * FRAME, key_low)
            key_high = jnp.where(member, jnp.minimum(starts[c] + block * FRAME + FRAME, ends[c]), key_high)
            row_low = jnp.where(member, starts[c] + jnp.maximum(block - reach_ref[0, c], 0) * FRAME, row_low)
            row_high = jnp.where(member, ends[c], row_high)
            first = last
            step_lane = jnp.where(ids == c, step_ref[0, c], step_lane)
            clip_gates.append(
                jnp.sum(
                    jnp.where(step_of == step_ref[0, c], head_gate.astype(jnp.float32), 0.0),
                    axis=0, keepdims=True,
                )
            )
        step_hot[...] = (
            lax.broadcasted_iota(jnp.int32, (STEPS, SEQ), 0) == step_lane
        ).astype(jnp.bfloat16)
        number = lax.broadcasted_iota(jnp.int32, (ROWS, HEAD), 0)

        def layout(n, carry):
            base = pl.multiple_of(n * ROWS, ROWS)
            rows = pl.ds(base, ROWS)
            index = number + base
            wide[rows, U0 : U0 + HEAD] = jnp.where((index >= key_low) & (index < key_high), 1.0, 0.0).astype(jnp.bfloat16)
            wide[rows, ONE0 : ONE0 + HEAD] = jnp.ones((ROWS, HEAD), jnp.bfloat16)
            units[rows, :] = jnp.where((index >= row_low) & (index < row_high), 0.0, NEGATIVE).astype(jnp.bfloat16)
            gate = clip_gates[CLIPS - 1]
            for c in reversed(range(CLIPS - 1)):
                gate = jnp.where(index < ends[c], clip_gates[c], gate)
            gates[rows, :] = gate.astype(jnp.bfloat16)
            return carry

        lax.fori_loop(0, N_Z, layout, 0)

    wait_for(slot_dst.at[pl.ds(0, 31)], sl_recv)
    row_of = lax.broadcasted_iota(jnp.int32, (TOK, SLOTS), 0).astype(jnp.float32)
    placing = []
    for half in range(2):
        slot_row = jnp.sum(slot_dst[half * N_DP : (half + 1) * N_DP], axis=0)
        placing.append(jnp.where(row_of == slot_row, 1.0, 0.0).astype(jnp.bfloat16))
    here = pl.ds(pl.multiple_of(z * ROWS, ROWS), ROWS)
    for k in range(CHUNKS):
        wait_for(recv.at[pl.ds(k * 512, 31 * CAP), :], a_recv.at[k])
        z_to = lax.rem(z + order_at(z, skip, k), N_Z)
        for half in range(2):
            low = k * 512 + half * SLOTS
            bsend[k * ROWS + half * TOK : k * ROWS + (half + 1) * TOK, :] = dot(
                placing[half], recv[low : low + SLOTS, :], ((1,), (0,))
            ).astype(jnp.bfloat16)
        piece = pl.ds(k * ROWS, ROWS)

        @pl.when(z_to != z)
        def _():
            blk_to = z_to * 2 + x_lo
            remote(
                bsend.at[piece, 0 : 2 * HEAD], wide.at[here, Q0:U0], b_send, b_recv, dp, blk_to
            ).start()
            remote(
                bsend.at[piece, 2 * HEAD : SPAN], wide.at[here, V0:ONE0], b_send, b_recv, dp, blk_to
            ).start()

        @pl.when(z_to == z)
        def _():
            wide[here, Q0:U0] = bsend[piece, 0 : 2 * HEAD]
            wide[here, V0:ONE0] = bsend[piece, 2 * HEAD : SPAN]

    def zs_rows(n, which=0):
        base = lax.rem(z + RETURNS[n], N_Z) * ROWS
        return pl.ds(pl.multiple_of(which * SEQ + base, ROWS), ROWS)

    relayed = lax.rem(z, 4) == skip_of(core, 1 - x_lo)
    relayed_head = (1 - x_lo) * CHUNKS + rank_of(z, skip_of(core, 1 - x_lo))

    def back_place(which, of_head):
        target, column = ((att_ref, 0), (qkvg_ref, 0), (qkvg_ref, 1), (qkvg_ref, 2))[which]
        return target.at[:, pl.ds(pl.multiple_of(column * WIDTH + of_head * HEAD, HEAD), HEAD)]

    def back_block(which, z_to, half):
        return cbuf.at[pl.ds(pl.multiple_of(which * SEQ + z_to * ROWS + half * TOK, TOK), TOK), :]

    def send_back(which, n):
        arrive = cq_recv if which else ca_recv
        z_to = lax.rem(z + RETURNS[n], N_Z)
        place = back_place(which, head)
        near = back_block(which, z_to, x_lo)
        far = back_block(which, z_to, 1 - x_lo)
        straight = remote(far, place, c_send, arrive, dp, z_to * 2 + 1 - x_lo)
        if RETURNS[n]:
            remote(near, place, c_send, arrive, dp, z_to * 2 + x_lo).start()
            by_relay = remote(far, far, c_send, hop.at[which * 8 + n], dp, blk_tos[1])
            pl.when(relayed)(by_relay.start)
            pl.when(jnp.logical_not(relayed))(straight.start)
        else:
            place[...] = near[...]
            straight.start()

    def pass_steps():
        mine = g2.at[halves[0]]
        for n in range(1, 16):
            remote(mine, mine, g3s, g3r, halves[n // 2] * 2 + cores[n % 2], blk).start()

    def pass_on(which, n):
        z_to = lax.rem(z + RETURNS[n], N_Z)
        block = back_block(which, z_to, x_lo)
        wait_for(block, hop.at[which * 8 + n])
        arrive = cq_recv if which else ca_recv
        remote(block, back_place(which, relayed_head), c_send, arrive, dp, z_to * 2 + x_lo).start()

    @pl.when(jnp.logical_not(is_host))
    def _():
        for which in range(2):
            for n in range(N_Z - 1):
                pass_on(which, n)
        for n in range(N_Z - 1):
            if n == GATE_AT:

                @pl.when(core == 1)
                def _():
                    wait_for(g2.at[halves[0]], g2r)
                    pass_steps()

            pass_on(2, n)
            pass_on(3, n)

    @pl.when(is_host)
    def _():
        wait_for(og.at[pl.ds(0, 15 * TOK), :], do_recv)
        grads[...] = (gates[...].astype(jnp.float32) * og[...].astype(jnp.float32)).astype(jnp.bfloat16)
        wait_for(recv.at[pl.ds(0, 7 * ROWS), :], b_recv)

        scores = (scores_a, scores_b)

        def score_tile(n, t, queries, top):
            keys = wide[t * TILE : (t + 1) * TILE, K0:V0]
            tile = dot(queries, keys, ((1,), (1,)))
            scores[n % 2][:, t * TILE : (t + 1) * TILE] = tile
            for u in range(TILE // HEAD):
                part = tile[:, u * HEAD : (u + 1) * HEAD]
                top = part if top is None else jnp.maximum(top, part)
            return top

        def query_rows(n):
            return jnp.concatenate([wide[zs_rows(n), Q0:K0], units[zs_rows(n), :]], axis=1)

        lane_of = lax.broadcasted_iota(jnp.int32, (ROWS, HEAD), 1)
        step_total = jnp.zeros((STEPS, HEAD), jnp.float32)
        top = None
        queries = query_rows(0)
        for t in range(SEQ // TILE):
            top = score_tile(0, t, queries, top)
        eye = jnp.where(
            lax.broadcasted_iota(jnp.int32, (HEAD, HEAD), 0) == lax.broadcasted_iota(jnp.int32, (HEAD, HEAD), 1), 1.0, 0.0
        ).astype(jnp.bfloat16)

        def split(rest):
            high = rest.astype(jnp.bfloat16)
            rest = rest - high.astype(jnp.float32)
            middle = rest.astype(jnp.bfloat16)
            return high, middle, (rest - middle.astype(jnp.float32)).astype(jnp.bfloat16)

        def finish_rows(n, summed, step_total):
            rows = zs_rows(n)
            inverse = 1.0 / summed[:, HEAD:]
            attention = summed[:, :HEAD] * inverse
            cbuf[zs_rows(n), :] = (gates[rows, :].astype(jnp.float32) * attention).astype(jnp.bfloat16)
            send_back(0, n)
            grad_out = grads[rows, :].astype(jnp.float32)
            row_delta = jnp.sum(grad_out * attention, axis=1, keepdims=True) * inverse
            grad_out = (grad_out * inverse).astype(jnp.bfloat16)
            high, middle, small = split(-row_delta)
            zero = jnp.zeros((ROWS, HEAD), jnp.bfloat16)
            grads_up[rows, 0:HEAD] = grad_out
            grads_up[rows, HEAD:] = jnp.where(
                lane_of == 0, high, jnp.where(lane_of == 1, middle, jnp.where(lane_of == 2, small, zero))
            )
            do_t[:, rows] = dot(eye, grad_out, ((1,), (1,))).astype(jnp.bfloat16)
            q_t[:, rows] = dot(eye, wide[rows, Q0:K0], ((1,), (1,))).astype(jnp.bfloat16)
            parts = jnp.concatenate(split(og[rows, :].astype(jnp.float32) * attention), axis=1)
            sums = dot(step_hot[:, rows], parts, ((1,), (0,)))
            return step_total + ((sums[:, 2 * HEAD :] + sums[:, HEAD : 2 * HEAD]) + sums[:, :HEAD])

        before = None
        for n in range(N_Z):
            rows = zs_rows(n)
            row_top = jnp.max(top, axis=1, keepdims=True)
            top = None
            if n + 1 < N_Z:
                queries = query_rows(n + 1)
            summed = None
            for t in range(SEQ // TILE):
                columns = slice(t * TILE, (t + 1) * TILE)
                if n + 1 < N_Z:
                    top = score_tile(n + 1, t, queries, top)
                parts = jnp.exp2((scores[n % 2][:, columns] - row_top) * SCALE2).astype(jnp.bfloat16)
                weights[rows, columns] = parts
                term = dot(parts, wide[columns, V0 : V0 + 2 * HEAD], ((1,), (0,)))
                summed = term if summed is None else summed + term
                if t == 0 and before is not None:
                    step_total = finish_rows(n - 1, before, step_total)
            before = summed
        step_total = finish_rows(N_Z - 1, before, step_total)

        for p in range(8):
            gpart[p] = step_total[8 * p : 8 * p + 8, :]
        owner_blk = jnp.where(core == 1, blk, other_blk)
        for n in range(8):
            copy = remote(
                gpart.at[halves[n]], g1.at[dp], g1s, g1r, halves[n] * 2 + 1, owner_blk
            )
            if n:
                copy.start()
            else:
                pl.when(core == 0)(copy.start)

        @pl.when(core == 1)
        def _():
            g1[pl.ds(dp, 1)] = gpart[pl.ds(halves[0], 1)]

        for n in range(N_Z):
            rows = zs_rows(n)
            up = grads_up[rows, :]
            for t in range(SEQ // TILE):
                columns = slice(t * TILE, (t + 1) * TILE)
                prob_grad = dot(up, wide[columns, V0 : V0 + 2 * HEAD], ((1,), (1,)))
                dscore[rows, columns] = (weights[rows, columns].astype(jnp.float32) * prob_grad).astype(jnp.bfloat16)
            query_grad = dot(dscore[rows, :], wide[:, K0:U0], ((1,), (0,))) * SCALE
            cbuf[zs_rows(n, 1), :] = query_grad.astype(jnp.bfloat16)
            send_back(1, n)

        def finish_steps():
            wait_for(g1.at[pl.ds(0, 15)], g1r)
            g2[halves[0], head] = jnp.sum(g1[...], axis=0)
            mine = g2.at[halves[0], head]
            for n in range(1, N_BLK):
                remote(mine, mine, g2s, g2r, dp, lax.rem(blk + n, N_BLK)).start()

        @pl.when(core == 1)
        def _():
            finish_steps()

        for n in range(N_Z):
            columns = zs_rows(n)
            key_grad = dot(q_t[...], dscore[:, columns], ((1,), (0,))) * SCALE
            cbuf[zs_rows(n, 2), :] = key_grad.T.astype(jnp.bfloat16)
            value_grad = dot(do_t[...], weights[:, columns], ((1,), (0,)))
            cbuf[zs_rows(n, 3), :] = value_grad.T.astype(jnp.bfloat16)

            send_back(2, n)
            send_back(3, n)

    @pl.when((core == 1) & is_host)
    def _():
        wait_for(g2.at[halves[0], pl.ds(0, 11)], g2r)
        pass_steps()

    wait_for(slot_dst.at[pl.ds(0, 31)], sl_send)
    wait_for(stage.at[pl.ds(0, 186 * CAP), :], a_send)
    @pl.when(core == 0)
    def _():
        wait_for(g2.at[pl.ds(0, 8)], g3r)

    @pl.when(core == 1)
    def _():
        wait_for(g2.at[pl.ds(0, 7)], g3r)

    for p in range(8):
        for h in range(HEADS):
            gg_ref[8 * p : 8 * p + 8, h * HEAD : (h + 1) * HEAD] = g2[p, h]

    @pl.when(is_host)
    def _():
        wait_for(grad_ref.at[:, pl.ds(0, 11 * HEAD)], do_send)
        wait_for(bsend.at[pl.ds(0, 5 * ROWS), :], b_send)

        @pl.when(core == 0)
        def _():
            wait_for(gpart.at[pl.ds(0, 8)], g1s)

        @pl.when(core == 1)
        def _():
            wait_for(gpart.at[pl.ds(0, 7)], g1s)
            wait_for(g1.at[pl.ds(0, 15)], g2s)

        wait_for(att_ref.at[:, pl.ds(0, 11 * HEAD)], ca_recv)
        wait_for(qkvg_ref.at[:, pl.ds(0, 33 * HEAD)], cq_recv)
        wait_for(cbuf.at[pl.ds(0, 60 * TOK), :], c_send)

    @pl.when(jnp.logical_not(is_host))
    def _():
        wait_for(grad_ref, do_send)
        wait_for(bsend, b_send)
        wait_for(cbuf.at[pl.ds(0, 28 * TOK), :], c_send)
        wait_for(att_ref, ca_recv)
        wait_for(qkvg_ref, cq_recv)

    @pl.when(core == 1)
    def _():
        wait_for(stage.at[pl.ds(0, 960), :], g3s)


def settle(a, b, c, a_out, b_out, c_out):
    a_out[...] = a[...]
    b_out[...] = b[...]
    c_out[...] = c[...]


def local(rows_in, slot_rows, clip_ids, clip_reach, clip_step, gate_table, out_grad):
    vmem = pl.BlockSpec(memory_space=pltpu.VMEM)
    smem = pl.BlockSpec(memory_space=pltpu.SMEM)
    bf16, f32 = jnp.bfloat16, jnp.float32
    sem = pltpu.SemaphoreType.DMA
    attended, qkv_grad, gate_grad = pl.pallas_call(
        kernel,
        out_shape=(
            jax.ShapeDtypeStruct((TOK, WIDTH), bf16),
            jax.ShapeDtypeStruct((TOK, 3 * WIDTH), bf16),
            jax.ShapeDtypeStruct((STEPS, WIDTH), f32),
        ),
        in_specs=[pl.BlockSpec(memory_space=pl.ANY), vmem, vmem, smem, smem, vmem, vmem],
        out_specs=(vmem, vmem, vmem),
        scratch_shapes=[
            pltpu.VMEM((8, 2, CAP, 3 * WIDTH), bf16),
            sem,
            pltpu.VMEM((CHUNKS * 2 * N_DP * CAP, SPAN), bf16),
            pltpu.VMEM((CHUNKS * 2 * SLOTS, SPAN), bf16),
            pltpu.VMEM((N_DP, 1, SLOTS), f32),
            pltpu.VMEM((2 * N_DP, 1, SLOTS), f32),
            pltpu.VMEM((CHUNKS * ROWS, SPAN), bf16),
            pltpu.VMEM((SEQ, 5 * HEAD), bf16),
            pltpu.VMEM((SEQ, HEAD), bf16),
            pltpu.VMEM((SEQ, HEAD), bf16),
            pltpu.VMEM((SEQ, HEAD), bf16),
            pltpu.VMEM((SEQ, HEAD), bf16),
            pltpu.VMEM((SEQ, 2 * HEAD), bf16),
            pltpu.VMEM((STEPS, SEQ), bf16),
            pltpu.VMEM((SEQ, SEQ), bf16),
            pltpu.VMEM((SEQ, SEQ), bf16),
            pltpu.VMEM((ROWS, SEQ), f32),
            pltpu.VMEM((ROWS, SEQ), f32),
            pltpu.VMEM((HEAD, SEQ), bf16),
            pltpu.VMEM((HEAD, SEQ), bf16),
            pltpu.VMEM((4 * SEQ, HEAD), bf16),
            pltpu.VMEM((8, 8, HEAD), f32),
            pltpu.VMEM((N_DP, 8, HEAD), f32),
            pltpu.VMEM((8, HEADS, 8, HEAD), f32),
            sem, sem((CHUNKS,)), sem, sem, sem, sem, sem, sem, sem, sem, sem,
            sem, sem, sem, sem, sem, sem, sem((32,)),
        ],
        compiler_params=pltpu.CompilerParams(
            collective_id=0, has_side_effects=True, vmem_limit_bytes=56 * 2**20
        ),
        name="attention",
    )(
        rows_in.reshape(8, 2, CAP, 3 * WIDTH),
        slot_rows.reshape(N_DP, CAP),
        clip_ids,
        clip_reach,
        clip_step,
        gate_table,
        out_grad[0],
    )
    shapes = [x.shape for x in (attended, qkv_grad, gate_grad)]
    blocks = [pl.BlockSpec((rows // 2, columns), lambda i: (i, 0)) for rows, columns in shapes]
    attended, qkv_grad, gate_grad = pl.pallas_call(
        settle,
        grid=(2,),
        out_shape=tuple(jax.ShapeDtypeStruct(x.shape, x.dtype) for x in (attended, qkv_grad, gate_grad)),
        in_specs=blocks,
        out_specs=tuple(blocks),
        name="settle",
    )(attended, qkv_grad, gate_grad)
    return attended[None], qkv_grad[None], gate_grad


def solution(mesh):
    return jax.shard_map(
        local,
        mesh=mesh,
        in_specs=(
            P("dp", "blk", None, None, None),
            P("dp", "blk", None, None),
            P("dp", None),
            P("dp", None),
            P("dp", None),
            P(),
            P("dp", "blk", None),
        ),
        out_specs=(P("dp", "blk", None), P("dp", "blk", None), P()),
        check_vma=False,
    )
```

```python
import math

import jax
import jax.numpy as jnp
from jax import lax
from jax.experimental import pallas as pl
from jax.experimental.pallas import tpu as pltpu
from jax.sharding import PartitionSpec as P

MESH = pl.DeviceIdType.MESH
HEAD = 128
HEADS = 12
WIDTH = HEADS * HEAD
TOK = 128
SEQ = 2048
FRAME = 128
CLIPS = 4
STEPS = 64
CAP = 16
N_DP = 16
N_BLK = 16
N_Z = 8
CHUNKS = 6
SPAN = 3 * HEAD
ROWS = 256
TILE = 512
SLOTS = N_DP * CAP
SCALE = 1.0 / math.sqrt(HEAD)
SCALE2 = SCALE * math.log2(math.e)
NEGATIVE = -1e30
Q0, K0, U0, V0, ONE0 = 0, 128, 256, 384, 512
GATE_AT = 4
RETURNS = (1, 7, 2, 6, 3, 5, 4, 0)
ORDER = ((3, 5, 2, 6, 1, 7), (4, 3, 2, 6, 7, 0), (4, 3, 5, 1, 7, 0), (4, 5, 2, 6, 1, 0))


def skip_of(core, x_lo):
    return 3 - 2 * core - x_lo


def order_at(z, skip, k):
    u = lax.rem(skip - z + 8, 4)
    last = jnp.where(u == 2, ORDER[2][k], ORDER[3][k])
    return jnp.where(u == 0, ORDER[0][k], jnp.where(u == 1, ORDER[1][k], last))


def rank_of(z, skip):
    part = lax.rem(z, 4)
    return (z // 4) * 3 + part - jnp.where(part > skip, 1, 0)


def z_of_rank(rank, skip):
    part = lax.rem(rank, 3)
    return (rank // 3) * 4 + part + jnp.where(part >= skip, 1, 0)


def dot(a, b, dims):
    return lax.dot_general(a, b, (dims, ((), ())), preferred_element_type=jnp.float32)


def wait_for(ref, sem):
    pltpu.make_async_copy(ref, ref, sem).wait()


def kernel(
    rows_ref, slot_ref, clip_ref, reach_ref, step_ref, gate_ref, grad_ref,
    att_ref, qkvg_ref, gg_ref,
    rows_here, in_sem, stage, recv, slot_src, slot_dst, bsend, wide, og, units, gates, grads, grads_up, step_hot,
    weights, dscore, scores_a, scores_b, q_t, do_t, cbuf, gpart, g1, g2,
    a_send, a_recv, sl_send, sl_recv, do_send, do_recv, b_send, b_recv, c_send, ca_recv, cq_recv,
    g1s, g1r, g2s, g2r, g3s, g3r, hop,
):
    for n in range(8):
        pltpu.make_async_copy(rows_ref.at[n], rows_here.at[n], in_sem).start()
    dp = lax.axis_index("dp")
    blk = lax.axis_index("blk")
    far_x = dp // 8
    y = lax.rem(dp // 2, 4)
    core = lax.rem(dp, 2)
    z = blk // 2
    x_lo = lax.rem(blk, 2)
    skip = skip_of(core, x_lo)
    is_host = lax.rem(z, 4) != skip
    rank = rank_of(z, skip)
    head = x_lo * CHUNKS + rank
    other_core = 1 - core
    other_z = z_of_rank(rank, skip_of(other_core, x_lo))
    other_blk = other_z * 2 + x_lo

    def remote(src, dst, send, arrive, dp_to, blk_to):
        return pltpu.make_async_remote_copy(
            src_ref=src, dst_ref=dst, send_sem=send, recv_sem=arrive,
            device_id=(dp_to, blk_to), device_id_type=MESH,
        )

    barrier = pltpu.get_barrier_semaphore()

    def greet(dp_to, blk_to):
        pl.semaphore_signal(barrier, inc=1, device_id=(dp_to, blk_to), device_id_type=MESH)

    halves = []
    for n in range(8):
        halves.append(lax.rem(far_x + n // 4, 2) * 4 + lax.rem(y + n % 4, 4))
    x_tos = (x_lo, 1 - x_lo)
    blk_tos = (z * 2 + x_lo, z * 2 + 1 - x_lo)
    plane = [(n, 0) for n in range(1, 16)] + [(n, 1) for n in range(16)]
    cores = (core, 1 - core)
    for n, other in plane:
        greet(halves[n // 2] * 2 + cores[other], blk_tos[n % 2])
    for n in range(1, N_BLK):
        greet(dp, lax.rem(blk + n, N_BLK))

    @pl.when(is_host)
    def _():
        for n in range(8):
            greet(halves[n] * 2 + other_core, other_blk)

    own = core * 8 + dp // 2

    def stage_base(k, x_to, core_to):
        return ((k * 2 + x_to) * 2 + core_to) * 128

    wait_for(rows_here, in_sem)
    for core_to in (0, 1):
        for k in range(CHUNKS):
            for x_to in (0, 1):
                far = skip_of(core_to, x_to)
                z_to = lax.rem(z + order_at(z, far, k), N_Z)
                column = pl.multiple_of((x_to * CHUNKS + rank_of(z_to, far)) * HEAD, HEAD)
                base = stage_base(k, x_to, core_to)
                for part in range(3):
                    stage[base : base + 128, part * HEAD : (part + 1) * HEAD] = rows_here[
                        :, core_to, :, pl.ds(part * WIDTH + column, HEAD)
                    ].reshape(128, HEAD)

    lane = lax.broadcasted_iota(jnp.int32, (CAP, SLOTS), 1)
    spread = (lane == lax.broadcasted_iota(jnp.int32, (CAP, SLOTS), 0) + dp * CAP).astype(jnp.bfloat16)
    slots = dot(slot_ref[...].astype(jnp.bfloat16), spread, ((1,), (0,)))
    for q in range(N_DP):
        slot_src[q] = slots[q : q + 1, :]
    source = x_lo * N_DP + dp
    slot_dst[pl.ds(source, 1)] = slot_src[pl.ds(dp, 1)]
    for k in range(CHUNKS):
        recv[pl.ds(pl.multiple_of(k * 512 + source * CAP, CAP), CAP), :] = stage[
            pl.ds(pl.multiple_of(((k * 2 + x_lo) * 16 + own) * CAP, CAP), CAP), :
        ]

    @pl.when(is_host)
    def _():
        og[pl.ds(pl.multiple_of(blk * TOK, TOK), TOK), :] = grad_ref[
            :, pl.ds(pl.multiple_of(head * HEAD, HEAD), HEAD)
        ]
        pl.semaphore_wait(barrier, 2 * N_DP - 1 + N_BLK - 1 + N_DP // 2)

    @pl.when(jnp.logical_not(is_host))
    def _():
        pl.semaphore_wait(barrier, 2 * N_DP - 1 + N_BLK - 1)

    for n, other in plane:
        dp_to = halves[n // 2] * 2 + cores[other]
        remote(slot_src.at[dp_to], slot_dst.at[source], sl_send, sl_recv, dp_to, blk_tos[n % 2]).start()

    source_row = source * CAP
    targets = [x_tos[n % 2] * 256 + halves[n // 2] * CAP for n in range(16)]

    for k in range(CHUNKS):
        for core_to in (0, 1):
            for n in range(16):
                copy = remote(
                    stage.at[pl.ds(pl.multiple_of(targets[n] + (k * 512 + core_to * 128), CAP), CAP), :],
                    recv.at[pl.ds(pl.multiple_of(source_row + k * 512, CAP), CAP), :],
                    a_send, a_recv.at[k], halves[n // 2] * 2 + core_to, blk_tos[n % 2],
                )
                if n:
                    copy.start()
                else:
                    pl.when(core != core_to)(copy.start)

            if core_to == 0:
                for x_to in (0, 1):
                    far = skip_of(core, x_to)
                    z_to = lax.rem(z + order_at(z, far, k), N_Z)
                    column = (x_to * CHUNKS + rank_of(z_to, far)) * HEAD
                    blk_to = z_to * 2 + x_to

                    @pl.when(blk_to != blk)
                    def _():
                        remote(
                            grad_ref.at[:, pl.ds(pl.multiple_of(column, HEAD), HEAD)],
                            og.at[pl.ds(pl.multiple_of(blk * TOK, TOK), TOK), :],
                            do_send, do_recv, dp, blk_to,
                        ).start()

    ids = clip_ref[...]
    ends = []
    for c in range(CLIPS):
        ends.append(
            jnp.sum(jnp.where(ids <= c, 1.0, 0.0), axis=1, keepdims=True).astype(jnp.int32)
        )
    starts = [jnp.zeros((1, 1), jnp.int32)] + ends[:-1]

    @pl.when(is_host)
    def _():
        head_gate = gate_ref[:, pl.ds(pl.multiple_of(head * HEAD, HEAD), HEAD)]
        unit = lax.broadcasted_iota(jnp.int32, (1, HEAD), 1)
        key_low = jnp.full((1, HEAD), SEQ, jnp.int32)
        key_high = jnp.full((1, HEAD), SEQ, jnp.int32)
        row_low = jnp.full((1, HEAD), SEQ, jnp.int32)
        row_high = jnp.full((1, HEAD), SEQ, jnp.int32)
        step_lane = jnp.zeros((1, SEQ), jnp.int32)
        step_of = lax.broadcasted_iota(jnp.int32, (STEPS, HEAD), 0)
        clip_gates = []
        first = jnp.zeros((1, 1), jnp.int32)
        for c in range(CLIPS):
            last = first + (ends[c] - starts[c] + FRAME - 1) // FRAME
            member = (unit >= first) & (unit < last)
            block = unit - first
            key_low = jnp.where(member, starts[c] + block * FRAME, key_low)
            key_high = jnp.where(member, jnp.minimum(starts[c] + block * FRAME + FRAME, ends[c]), key_high)
            row_low = jnp.where(member, starts[c] + jnp.maximum(block - reach_ref[0, c], 0) * FRAME, row_low)
            row_high = jnp.where(member, ends[c], row_high)
            first = last
            step_lane = jnp.where(ids == c, step_ref[0, c], step_lane)
            clip_gates.append(
                jnp.sum(
                    jnp.where(step_of == step_ref[0, c], head_gate.astype(jnp.float32), 0.0),
                    axis=0, keepdims=True,
                )
            )
        step_hot[...] = (
            lax.broadcasted_iota(jnp.int32, (STEPS, SEQ), 0) == step_lane
        ).astype(jnp.bfloat16)
        number = lax.broadcasted_iota(jnp.int32, (ROWS, HEAD), 0)

        def layout(n, carry):
            base = pl.multiple_of(n * ROWS, ROWS)
            rows = pl.ds(base, ROWS)
            index = number + base
            wide[rows, U0 : U0 + HEAD] = jnp.where((index >= key_low) & (index < key_high), 1.0, 0.0).astype(jnp.bfloat16)
            wide[rows, ONE0 : ONE0 + HEAD] = jnp.ones((ROWS, HEAD), jnp.bfloat16)
            units[rows, :] = jnp.where((index >= row_low) & (index < row_high), 0.0, NEGATIVE).astype(jnp.bfloat16)
            gate = clip_gates[CLIPS - 1]
            for c in reversed(range(CLIPS - 1)):
                gate = jnp.where(index < ends[c], clip_gates[c], gate)
            gates[rows, :] = gate.astype(jnp.bfloat16)
            return carry

        lax.fori_loop(0, N_Z, layout, 0)

    wait_for(slot_dst.at[pl.ds(0, 31)], sl_recv)
    row_of = lax.broadcasted_iota(jnp.int32, (TOK, SLOTS), 0).astype(jnp.float32)
    placing = []
    for half in range(2):
        slot_row = jnp.sum(slot_dst[half * N_DP : (half + 1) * N_DP], axis=0)
        placing.append(jnp.where(row_of == slot_row, 1.0, 0.0).astype(jnp.bfloat16))
    here = pl.ds(pl.multiple_of(z * ROWS, ROWS), ROWS)
    for k in range(CHUNKS):
        wait_for(recv.at[pl.ds(k * 512, 31 * CAP), :], a_recv.at[k])
        z_to = lax.rem(z + order_at(z, skip, k), N_Z)
        for half in range(2):
            low = k * 512 + half * SLOTS
            bsend[k * ROWS + half * TOK : k * ROWS + (half + 1) * TOK, :] = dot(
                placing[half], recv[low : low + SLOTS, :], ((1,), (0,))
            ).astype(jnp.bfloat16)
        piece = pl.ds(k * ROWS, ROWS)

        @pl.when(z_to != z)
        def _():
            blk_to = z_to * 2 + x_lo
            remote(
                bsend.at[piece, 0 : 2 * HEAD], wide.at[here, Q0:U0], b_send, b_recv, dp, blk_to
            ).start()
            remote(
                bsend.at[piece, 2 * HEAD : SPAN], wide.at[here, V0:ONE0], b_send, b_recv, dp, blk_to
            ).start()

        @pl.when(z_to == z)
        def _():
            wide[here, Q0:U0] = bsend[piece, 0 : 2 * HEAD]
            wide[here, V0:ONE0] = bsend[piece, 2 * HEAD : SPAN]

    def zs_rows(n, which=0):
        base = lax.rem(z + RETURNS[n], N_Z) * ROWS
        return pl.ds(pl.multiple_of(which * SEQ + base, ROWS), ROWS)

    relayed = lax.rem(z, 4) == skip_of(core, 1 - x_lo)
    relayed_head = (1 - x_lo) * CHUNKS + rank_of(z, skip_of(core, 1 - x_lo))

    def back_place(which, of_head):
        target, column = ((att_ref, 0), (qkvg_ref, 0), (qkvg_ref, 1), (qkvg_ref, 2))[which]
        return target.at[:, pl.ds(pl.multiple_of(column * WIDTH + of_head * HEAD, HEAD), HEAD)]

    def back_block(which, z_to, half):
        return cbuf.at[pl.ds(pl.multiple_of(which * SEQ + z_to * ROWS + half * TOK, TOK), TOK), :]

    def send_back(which, n):
        arrive = cq_recv if which else ca_recv
        z_to = lax.rem(z + RETURNS[n], N_Z)
        place = back_place(which, head)
        near = back_block(which, z_to, x_lo)
        far = back_block(which, z_to, 1 - x_lo)
        straight = remote(far, place, c_send, arrive, dp, z_to * 2 + 1 - x_lo)
        if RETURNS[n]:
            remote(near, place, c_send, arrive, dp, z_to * 2 + x_lo).start()
            by_relay = remote(far, far, c_send, hop.at[which * 8 + n], dp, blk_tos[1])
            pl.when(relayed)(by_relay.start)
            pl.when(jnp.logical_not(relayed))(straight.start)
        else:
            place[...] = near[...]
            straight.start()

    def pass_steps():
        mine = g2.at[halves[0]]
        for n in range(1, 16):
            remote(mine, mine, g3s, g3r, halves[n // 2] * 2 + cores[n % 2], blk).start()

    def pass_on(which, n):
        z_to = lax.rem(z + RETURNS[n], N_Z)
        block = back_block(which, z_to, x_lo)
        wait_for(block, hop.at[which * 8 + n])
        arrive = cq_recv if which else ca_recv
        remote(block, back_place(which, relayed_head), c_send, arrive, dp, z_to * 2 + x_lo).start()

    @pl.when(jnp.logical_not(is_host))
    def _():
        for which in range(2):
            for n in range(N_Z - 1):
                pass_on(which, n)
        for n in range(N_Z - 1):
            if n == GATE_AT:

                @pl.when(core == 1)
                def _():
                    wait_for(g2.at[halves[0]], g2r)
                    pass_steps()

            pass_on(2, n)
            pass_on(3, n)

    @pl.when(is_host)
    def _():
        wait_for(og.at[pl.ds(0, 15 * TOK), :], do_recv)
        grads[...] = (gates[...].astype(jnp.float32) * og[...].astype(jnp.float32)).astype(jnp.bfloat16)
        wait_for(recv.at[pl.ds(0, 7 * ROWS), :], b_recv)

        scores = (scores_a, scores_b)

        def score_tile(n, t, queries, top):
            keys = wide[t * TILE : (t + 1) * TILE, K0:V0]
            tile = dot(queries, keys, ((1,), (1,)))
            scores[n % 2][:, t * TILE : (t + 1) * TILE] = tile
            for u in range(TILE // HEAD):
                part = tile[:, u * HEAD : (u + 1) * HEAD]
                top = part if top is None else jnp.maximum(top, part)
            return top

        def query_rows(n):
            return jnp.concatenate([wide[zs_rows(n), Q0:K0], units[zs_rows(n), :]], axis=1)

        lane_of = lax.broadcasted_iota(jnp.int32, (ROWS, HEAD), 1)
        step_total = jnp.zeros((STEPS, HEAD), jnp.float32)
        top = None
        queries = query_rows(0)
        for t in range(SEQ // TILE):
            top = score_tile(0, t, queries, top)
        eye = jnp.where(
            lax.broadcasted_iota(jnp.int32, (HEAD, HEAD), 0) == lax.broadcasted_iota(jnp.int32, (HEAD, HEAD), 1), 1.0, 0.0
        ).astype(jnp.bfloat16)

        def split(rest):
            high = rest.astype(jnp.bfloat16)
            rest = rest - high.astype(jnp.float32)
            middle = rest.astype(jnp.bfloat16)
            return high, middle, (rest - middle.astype(jnp.float32)).astype(jnp.bfloat16)

        def finish_rows(n, summed, step_total):
            rows = zs_rows(n)
            inverse = 1.0 / summed[:, HEAD:]
            attention = summed[:, :HEAD] * inverse
            cbuf[zs_rows(n), :] = (gates[rows, :].astype(jnp.float32) * attention).astype(jnp.bfloat16)
            send_back(0, n)
            grad_out = grads[rows, :].astype(jnp.float32)
            row_delta = jnp.sum(grad_out * attention, axis=1, keepdims=True) * inverse
            grad_out = (grad_out * inverse).astype(jnp.bfloat16)
            high, middle, small = split(-row_delta)
            zero = jnp.zeros((ROWS, HEAD), jnp.bfloat16)
            grads_up[rows, 0:HEAD] = grad_out
            grads_up[rows, HEAD:] = jnp.where(
                lane_of == 0, high, jnp.where(lane_of == 1, middle, jnp.where(lane_of == 2, small, zero))
            )
            do_t[:, rows] = dot(eye, grad_out, ((1,), (1,))).astype(jnp.bfloat16)
            q_t[:, rows] = dot(eye, wide[rows, Q0:K0], ((1,), (1,))).astype(jnp.bfloat16)
            parts = jnp.concatenate(split(og[rows, :].astype(jnp.float32) * attention), axis=1)
            sums = dot(step_hot[:, rows], parts, ((1,), (0,)))
            return step_total + ((sums[:, 2 * HEAD :] + sums[:, HEAD : 2 * HEAD]) + sums[:, :HEAD])

        before = None
        for n in range(N_Z):
            rows = zs_rows(n)
            row_top = jnp.max(top, axis=1, keepdims=True)
            top = None
            if n + 1 < N_Z:
                queries = query_rows(n + 1)
            summed = None
            for t in range(SEQ // TILE):
                columns = slice(t * TILE, (t + 1) * TILE)
                if n + 1 < N_Z:
                    top = score_tile(n + 1, t, queries, top)
                parts = jnp.exp2((scores[n % 2][:, columns] - row_top) * SCALE2).astype(jnp.bfloat16)
                weights[rows, columns] = parts
                term = dot(parts, wide[columns, V0 : V0 + 2 * HEAD], ((1,), (0,)))
                summed = term if summed is None else summed + term
                if t == 0 and before is not None:
                    step_total = finish_rows(n - 1, before, step_total)
            before = summed
        step_total = finish_rows(N_Z - 1, before, step_total)

        for p in range(8):
            gpart[p] = step_total[8 * p : 8 * p + 8, :]
        owner_blk = jnp.where(core == 1, blk, other_blk)
        for n in range(8):
            copy = remote(
                gpart.at[halves[n]], g1.at[dp], g1s, g1r, halves[n] * 2 + 1, owner_blk
            )
            if n:
                copy.start()
            else:
                pl.when(core == 0)(copy.start)

        @pl.when(core == 1)
        def _():
            g1[pl.ds(dp, 1)] = gpart[pl.ds(halves[0], 1)]

        for n in range(N_Z):
            rows = zs_rows(n)
            up = grads_up[rows, :]
            for t in range(SEQ // TILE):
                columns = slice(t * TILE, (t + 1) * TILE)
                prob_grad = dot(up, wide[columns, V0 : V0 + 2 * HEAD], ((1,), (1,)))
                dscore[rows, columns] = (weights[rows, columns].astype(jnp.float32) * prob_grad).astype(jnp.bfloat16)
            query_grad = dot(dscore[rows, :], wide[:, K0:U0], ((1,), (0,))) * SCALE
            cbuf[zs_rows(n, 1), :] = query_grad.astype(jnp.bfloat16)
            send_back(1, n)

        def finish_steps():
            wait_for(g1.at[pl.ds(0, 15)], g1r)
            g2[halves[0], head] = jnp.sum(g1[...], axis=0)
            mine = g2.at[halves[0], head]
            for n in range(1, N_BLK):
                remote(mine, mine, g2s, g2r, dp, lax.rem(blk + n, N_BLK)).start()

        @pl.when(core == 1)
        def _():
            finish_steps()

        for n in range(N_Z):
            columns = zs_rows(n)
            key_grad = dot(q_t[...], dscore[:, columns], ((1,), (0,))) * SCALE
            cbuf[zs_rows(n, 2), :] = key_grad.T.astype(jnp.bfloat16)
            value_grad = dot(do_t[...], weights[:, columns], ((1,), (0,)))
            cbuf[zs_rows(n, 3), :] = value_grad.T.astype(jnp.bfloat16)

            send_back(2, n)
            send_back(3, n)

    @pl.when((core == 1) & is_host)
    def _():
        wait_for(g2.at[halves[0], pl.ds(0, 11)], g2r)
        pass_steps()

    wait_for(slot_dst.at[pl.ds(0, 31)], sl_send)
    wait_for(stage.at[pl.ds(0, 186 * CAP), :], a_send)
    @pl.when(core == 0)
    def _():
        wait_for(g2.at[pl.ds(0, 8)], g3r)

    @pl.when(core == 1)
    def _():
        wait_for(g2.at[pl.ds(0, 7)], g3r)

    for p in range(8):
        for h in range(HEADS):
            gg_ref[8 * p : 8 * p + 8, h * HEAD : (h + 1) * HEAD] = g2[p, h]

    @pl.when(is_host)
    def _():
        wait_for(grad_ref.at[:, pl.ds(0, 11 * HEAD)], do_send)
        wait_for(bsend.at[pl.ds(0, 5 * ROWS), :], b_send)

        @pl.when(core == 0)
        def _():
            wait_for(gpart.at[pl.ds(0, 8)], g1s)

        @pl.when(core == 1)
        def _():
            wait_for(gpart.at[pl.ds(0, 7)], g1s)
            wait_for(g1.at[pl.ds(0, 15)], g2s)

        wait_for(att_ref.at[:, pl.ds(0, 11 * HEAD)], ca_recv)
        wait_for(qkvg_ref.at[:, pl.ds(0, 33 * HEAD)], cq_recv)
        wait_for(cbuf.at[pl.ds(0, 60 * TOK), :], c_send)

    @pl.when(jnp.logical_not(is_host))
    def _():
        wait_for(grad_ref, do_send)
        wait_for(bsend, b_send)
        wait_for(cbuf.at[pl.ds(0, 28 * TOK), :], c_send)
        wait_for(att_ref, ca_recv)
        wait_for(qkvg_ref, cq_recv)

    @pl.when(core == 1)
    def _():
        wait_for(stage.at[pl.ds(0, 960), :], g3s)


def settle(a, b, c, a_out, b_out, c_out):
    a_out[...] = a[...]
    b_out[...] = b[...]
    c_out[...] = c[...]


def local(rows_in, slot_rows, clip_ids, clip_reach, clip_step, gate_table, out_grad):
    vmem = pl.BlockSpec(memory_space=pltpu.VMEM)
    smem = pl.BlockSpec(memory_space=pltpu.SMEM)
    bf16, f32 = jnp.bfloat16, jnp.float32
    sem = pltpu.SemaphoreType.DMA
    attended, qkv_grad, gate_grad = pl.pallas_call(
        kernel,
        out_shape=(
            jax.ShapeDtypeStruct((TOK, WIDTH), bf16),
            jax.ShapeDtypeStruct((TOK, 3 * WIDTH), bf16),
            jax.ShapeDtypeStruct((STEPS, WIDTH), f32),
        ),
        in_specs=[pl.BlockSpec(memory_space=pl.ANY), vmem, vmem, smem, smem, vmem, vmem],
        out_specs=(vmem, vmem, vmem),
        scratch_shapes=[
            pltpu.VMEM((8, 2, CAP, 3 * WIDTH), bf16),
            sem,
            pltpu.VMEM((CHUNKS * 2 * N_DP * CAP, SPAN), bf16),
            pltpu.VMEM((CHUNKS * 2 * SLOTS, SPAN), bf16),
            pltpu.VMEM((N_DP, 1, SLOTS), f32),
            pltpu.VMEM((2 * N_DP, 1, SLOTS), f32),
            pltpu.VMEM((CHUNKS * ROWS, SPAN), bf16),
            pltpu.VMEM((SEQ, 5 * HEAD), bf16),
            pltpu.VMEM((SEQ, HEAD), bf16),
            pltpu.VMEM((SEQ, HEAD), bf16),
            pltpu.VMEM((SEQ, HEAD), bf16),
            pltpu.VMEM((SEQ, HEAD), bf16),
            pltpu.VMEM((SEQ, 2 * HEAD), bf16),
            pltpu.VMEM((STEPS, SEQ), bf16),
            pltpu.VMEM((SEQ, SEQ), bf16),
            pltpu.VMEM((SEQ, SEQ), bf16),
            pltpu.VMEM((ROWS, SEQ), f32),
            pltpu.VMEM((ROWS, SEQ), f32),
            pltpu.VMEM((HEAD, SEQ), bf16),
            pltpu.VMEM((HEAD, SEQ), bf16),
            pltpu.VMEM((4 * SEQ, HEAD), bf16),
            pltpu.VMEM((8, 8, HEAD), f32),
            pltpu.VMEM((N_DP, 8, HEAD), f32),
            pltpu.VMEM((8, HEADS, 8, HEAD), f32),
            sem, sem((CHUNKS,)), sem, sem, sem, sem, sem, sem, sem, sem, sem,
            sem, sem, sem, sem, sem, sem, sem((32,)),
        ],
        compiler_params=pltpu.CompilerParams(
            collective_id=0, has_side_effects=True, vmem_limit_bytes=56 * 2**20
        ),
        name="attention",
    )(
        rows_in.reshape(8, 2, CAP, 3 * WIDTH),
        slot_rows.reshape(N_DP, CAP),
        clip_ids,
        clip_reach,
        clip_step,
        gate_table,
        out_grad[0],
    )
    shapes = [x.shape for x in (attended, qkv_grad, gate_grad)]
    blocks = [pl.BlockSpec((rows // 2, columns), lambda i: (i, 0)) for rows, columns in shapes]
    attended, qkv_grad, gate_grad = pl.pallas_call(
        settle,
        grid=(2,),
        out_shape=tuple(jax.ShapeDtypeStruct(x.shape, x.dtype) for x in (attended, qkv_grad, gate_grad)),
        in_specs=blocks,
        out_specs=tuple(blocks),
        name="settle",
    )(attended, qkv_grad, gate_grad)
    return attended[None], qkv_grad[None], gate_grad


def solution(mesh):
    return jax.shard_map(
        local,
        mesh=mesh,
        in_specs=(
            P("dp", "blk", None, None, None),
            P("dp", "blk", None, None),
            P("dp", None),
            P("dp", None),
            P("dp", None),
            P(),
            P("dp", "blk", None),
        ),
        out_specs=(P("dp", "blk", None), P("dp", "blk", None), P()),
        check_vma=False,
    )
```
